256 devices in a mesh: seq: 32 (over z_lo, y, core), tp: 8 (over x, z_hi).
Axes of the slice: x: 4, y: 4, z: 8 (z_hi: 2, z_lo: 4; z = z_hi * 4 + z_lo), core: 2. Of those that a mesh axis runs over, the one named last changes fastest.
Arguments:
- q_prefill: bfloat16 [2, 8192, 8, 512], P(None, 'seq', 'tp'), may hold values from -6 to 6
- kv_prefill: bfloat16 [2, 8192, 8, 256], P(None, 'seq', 'tp'), may hold values from -6 to 6
- prompt_len: int32 [2], replicated, may hold values from 4096 to 8192, as said below
- group_of: int32 [2], replicated, may hold values from 0 to 1, each once
- hidden: bfloat16 [4, 2, 8192], P(None, None, 'seq'), may hold values from -6 to 6
- norm_gain: float32 [8192], P('seq'), may hold values from 0.5 to 2
- w_qkv: bfloat16 [8192, 8, 768], P('seq', 'tp'), may hold values from -0.23204774 to 0.23204774
- w_out: bfloat16 [8, 512, 8192], P('tp', None, 'seq'), may hold values from -0.09375 to 0.09375
Outputs:
- attn_prefill: bfloat16 [2, 8192, 8, 512], P(None, 'seq', 'tp')
- cache_pages: bfloat16 [16384, 8, 256], P('seq', 'tp')
- decoded: bfloat16 [4, 2, 8192], P(None, None, 'seq')
The draws below stay inside these ranges and needn't reach their ends.
Inputs may be any that keep to these rules, and one draw needn't show every extreme that they name: `prompt_len`: one prompt of every draw is 8192 long.
All inputs are finite; a program needn't handle non-finite values.
Results may differ from the reference program's by a relative error of at most 0.01.
Values may be sent and summed in bfloat16 or wider, within the bound.
A program may use at most 64 MiB of HBM per device.

```python
import math
import jax
import jax.numpy as jnp
from jax import lax

D = 8192
HEAD = 128
KV = 8
QPK = 4
NP = 2
TOK_DEV = 256
STEPS = 4
LEN = 8192
N_SEQ = 32


def prompt_lengths(key):
    key = jax.random.fold_in(key, 3)
    lengths = jax.random.randint(key, (NP,), LEN // 2, LEN + 1)
    longest = jax.random.randint(jax.random.fold_in(key, 4), (), 0, NP)
    return jnp.where(jnp.arange(NP) == longest, LEN, lengths).astype(jnp.int32)


def draw_q_prefill(key, part):
    own_key = jax.random.fold_in(key, 1)
    full_shape = (NP, LEN, KV, QPK * HEAD)
    base_draw = jnp.clip(jax.random.normal(own_key, full_shape, jnp.float32), -6.0, 6.0)
    return base_draw.astype(jnp.bfloat16)


def draw_kv_prefill(key, part):
    own_key = jax.random.fold_in(key, 2)
    full_shape = (NP, LEN, KV, 2 * HEAD)
    base_draw = jnp.clip(jax.random.normal(own_key, full_shape, jnp.float32), -6.0, 6.0)
    return base_draw.astype(jnp.bfloat16)


def draw_prompt_len(key, part):
    return prompt_lengths(key)


def draw_hidden(key, part):
    own_key = jax.random.fold_in(key, 6)
    full_shape = (STEPS, NP, D)
    values = jnp.clip(jax.random.normal(own_key, full_shape, jnp.float32), -6.0, 6.0)
    return values.astype(jnp.bfloat16)


def draw_w_qkv(key, part):
    own_key = jax.random.fold_in(key, 7)
    full_shape = (D, KV, (QPK + 2) * HEAD)
    spread = (D // 9) ** (-0.5)
    values = spread * jnp.clip(jax.random.normal(own_key, full_shape, jnp.float32), -6.0, 6.0)
    return values.astype(jnp.bfloat16)


def levels(rng, extent, split, smallest, high):
    def one(dim, blocks):
        draws = jax.random.uniform(jax.random.fold_in(jax.random.fold_in(rng, 6), dim), (blocks,), jnp.float32, smallest / len(split), high / len(split))
        return jnp.repeat(jnp.exp(draws), extent[dim] // blocks).reshape((-1,) + (1,) * (len(extent) - dim - 1))

    loudness = one(*split[0])
    for cut in split[1:]:
        loudness = loudness * one(*cut)
    return loudness


def bell_draw(key, dims, width, most, cuts=(), held_as=jnp.bfloat16):
    values = jax.random.normal(key, dims, jnp.float32) * width
    if len(cuts) > 0:
        values = levels(key, dims, cuts, -0.22, 0.18) * values
    return jnp.clip(values, min=-most, max=most).astype(held_as)


def setup_inputs(seed: int = 0) -> dict:
    keys = jax.random.split(jax.random.key(seed), 9)
    return {
        "q_prefill": draw_q_prefill(jax.random.fold_in(keys[8], 71), 0),
        "kv_prefill": draw_kv_prefill(jax.random.fold_in(keys[8], 71), 0),
        "prompt_len": draw_prompt_len(jax.random.fold_in(keys[8], 71), 0),
        "group_of": jax.random.permutation(keys[3], NP).astype(jnp.int32),
        "hidden": draw_hidden(jax.random.fold_in(keys[8], 71), 0),
        "norm_gain": jnp.clip(jnp.exp(math.log(2.0) - 1.3862944 * jax.random.uniform(keys[5], (D,), jnp.float32) ** levels(keys[5], (D,), ((0, 32),), -0.2, 0.2)), 0.5, 2.0),
        "w_qkv": draw_w_qkv(jax.random.fold_in(keys[8], 71), 0),
        "w_out": bell_draw(keys[7], (KV, QPK * HEAD, D), (KV * QPK * HEAD) ** -0.5, 0.09375, ((0, 8), (2, 32))),
    }


neg_big = -1e+30
norm_eps = 1e-05
rope_base = 500000.0

def rotate(vectors, position):
    half_size = vectors.shape[-1] // 2
    frequency = rope_base ** (-2.0 * jnp.arange(half_size, dtype=jnp.float32) / vectors.shape[-1])
    angle = position * frequency
    cosine_wave = jnp.cos(angle)
    sine_wave = jnp.sin(angle)
    front_half = vectors[..., :half_size]
    back_half = vectors[..., half_size:]
    return jnp.concatenate([front_half * cosine_wave - back_half * sine_wave, back_half * cosine_wave + front_half * sine_wave], axis=-1)

def prefill_item(operands):
    queries, keyvals, length = operands
    block_rows = min(LEN, 1024)
    block_count = LEN // block_rows
    score_scale = 1.0 / math.sqrt(HEAD)
    query_blocks = queries.reshape(block_count, block_rows, QPK, HEAD).astype(jnp.float32)
    key_blocks = keyvals.reshape(block_count, block_rows, 2 * HEAD).astype(jnp.float32)
    offsets = jnp.arange(block_rows, dtype=jnp.int32)

    def query_block(block_position_index):
        rows_here = lax.dynamic_index_in_dim(query_blocks, block_position_index, 0, keepdims=False)
        row_pos = block_position_index * block_rows + offsets

        def key_step(key_index, running):
            row_top, row_total, weighted = running
            keys_here = lax.dynamic_index_in_dim(key_blocks, key_index, 0, keepdims=False)
            key_pos = key_index * block_rows + offsets
            allowed = (key_pos[None, :] <= row_pos[:, None]) & (key_pos[None, :] < length)
            allowed = allowed[:, None, :]
            scores = jnp.einsum('rqd,nd->rqn', rows_here, keys_here[:, :HEAD]) * score_scale
            scores = jnp.where(allowed, scores, neg_big)
            new_top = jnp.maximum(row_top, lax.optimization_barrier(jnp.max(scores, axis=-1)))
            weight_matrices = jnp.exp(scores - new_top[..., None]) * allowed
            shrink = jnp.exp(row_top - new_top)
            row_total = row_total * shrink + lax.optimization_barrier(jnp.sum(weight_matrices, axis=-1))
            rounded = lax.optimization_barrier(weight_matrices.astype(jnp.bfloat16)).astype(jnp.float32)
            weighted = weighted * shrink[..., None] + jnp.einsum('rqn,nd->rqd', rounded, keys_here[:, HEAD:])
            return (new_top, row_total, weighted)
        start_state = (jnp.full((block_rows, QPK), neg_big, jnp.float32), jnp.zeros((block_rows, QPK), jnp.float32), jnp.zeros((block_rows, QPK, HEAD), jnp.float32))
        row_top, row_total, weighted = lax.fori_loop(0, block_position_index + 1, key_step, start_state)
        return (weighted / row_total[..., None]).astype(jnp.bfloat16)
    results = lax.map(query_block, jnp.arange(block_count, dtype=jnp.int32))
    return results.reshape(LEN, QPK * HEAD)

def reference(q_prefill, kv_prefill, prompt_len, group_of, hidden, norm_gain, w_qkv, w_out):
    queries = jnp.transpose(q_prefill.reshape(NP, LEN, KV, QPK, HEAD), (0, 2, 1, 3, 4)).reshape(NP * KV, LEN, QPK, HEAD)
    keyvals = jnp.transpose(kv_prefill, (0, 2, 1, 3)).reshape(NP * KV, LEN, 2 * HEAD)
    lengths = jnp.repeat(prompt_len, KV)
    attended = lax.map(prefill_item, (queries, keyvals, lengths))
    attn_prefill = jnp.transpose(attended.reshape(NP, KV, LEN, QPK * HEAD), (0, 2, 1, 3))
    group_size = N_SEQ // NP
    piece_rows = TOK_DEV // group_size
    prompt_ids = jnp.arange(NP, dtype=jnp.int32)
    prompt_of_group = lax.optimization_barrier(jnp.sum(jnp.where(group_of[None, :] == prompt_ids[:, None], prompt_ids[None, :], 0), axis=1)).astype(jnp.int32)
    by_group = jnp.take(kv_prefill, prompt_of_group, axis=0).reshape(NP, N_SEQ, group_size, piece_rows, KV, 2 * HEAD)
    cache_pages = jnp.transpose(by_group, (0, 2, 1, 3, 4, 5)).reshape(N_SEQ * NP * TOK_DEV, KV, 2 * HEAD)
    score_scale = 1.0 / math.sqrt(HEAD)
    norm_scale = norm_gain.astype(jnp.float32)
    w_flat = w_qkv.reshape(D, KV * (QPK + 2) * HEAD)
    out_flat = w_out.reshape(KV * QPK * HEAD, D)
    cache_keys = kv_prefill[..., :HEAD].astype(jnp.float32)
    cache_values = kv_prefill[..., HEAD:].astype(jnp.float32)
    cache_allowed = (jnp.arange(LEN, dtype=jnp.int32)[None, :] < prompt_len[:, None])[:, None, None, :]
    q_width = QPK * HEAD
    fresh_keys = []
    fresh_values = []
    outputs = []
    for step_index in range(STEPS):
        current = hidden[step_index].astype(jnp.float32)
        mean_square = lax.optimization_barrier(jnp.mean(current * current, axis=-1))
        scaled_in = (current * norm_scale).astype(jnp.bfloat16)
        projected = jnp.dot(scaled_in, w_flat, preferred_element_type=jnp.float32).reshape(NP, KV, (QPK + 2) * HEAD)
        projected = projected * lax.rsqrt(mean_square + norm_eps)[:, None, None]
        position = (prompt_len + step_index).astype(jnp.float32)
        query_new = rotate(projected[..., :q_width].reshape(NP, KV, QPK, HEAD), position[:, None, None, None]).astype(jnp.bfloat16)
        key_new = rotate(projected[..., q_width:q_width + HEAD], position[:, None, None]).astype(jnp.bfloat16)
        incoming_value = projected[..., q_width + HEAD:].astype(jnp.bfloat16)
        fresh_keys.append(key_new)
        fresh_values.append(incoming_value)
        query_wide = query_new.astype(jnp.float32)
        cache_scores = jnp.einsum('phqd,pnhd->phqn', query_wide, cache_keys) * score_scale
        cache_scores = jnp.where(cache_allowed, cache_scores, neg_big)
        recent_keys = jnp.stack(fresh_keys, 0).astype(jnp.float32)
        recent_values = jnp.stack(fresh_values, 0).astype(jnp.float32)
        recent_scores = jnp.einsum('phqd,sphd->phqs', query_wide, recent_keys) * score_scale
        row_top = jnp.maximum(lax.optimization_barrier(jnp.max(cache_scores, axis=-1)), lax.optimization_barrier(jnp.max(recent_scores, axis=-1)))
        cache_weights = jnp.exp(cache_scores - row_top[..., None]) * cache_allowed
        recent_weights = jnp.exp(recent_scores - row_top[..., None])
        row_total = lax.optimization_barrier(jnp.sum(cache_weights, axis=-1)) + lax.optimization_barrier(jnp.sum(recent_weights, axis=-1))
        weighted = jnp.einsum('phqn,pnhd->phqd', cache_weights, cache_values) + jnp.einsum('phqs,sphd->phqd', recent_weights, recent_values)
        attended_new = (weighted / row_total[..., None]).astype(jnp.bfloat16).reshape(NP, KV * q_width)
        head_mixed = jnp.dot(attended_new, out_flat, preferred_element_type=jnp.float32)
        outputs.append((current + head_mixed).astype(jnp.bfloat16))
    return (attn_prefill, cache_pages, jnp.stack(outputs, 0))
```

```python
import functools
import math

import jax
import jax.numpy as jnp
from jax import lax
from jax.experimental import pallas as pl
from jax.experimental.pallas import tpu as pltpu
from jax.sharding import PartitionSpec as P

MESH = pl.DeviceIdType.MESH
NEG = -1e30
EPS = 1e-05
BASE = 500000.0
ROWS = 256
BLOCK = 512
HD = 128
HEADS = 4
PART_A = 128
PART_B = BLOCK - PART_A
HALF_A, HALF_B = PART_A // 2, PART_B // 2
NY = 4
NZ = 4
NX = 4
BF16 = jnp.bfloat16
F32 = jnp.float32
NT = (((1,), (1,)), ((), ()))


def kernel(
    width,
    lens_ref, q_ref, kv_ref, hid_ref, gain_ref, wqkv_ref, wout_ref, cos_ref, sin_ref,
    attn_ref, dec_ref,
    blocks, q_in, q_scaled, acc, tops, o_in, o_out,
    proj_core, proj_y, proj_z, soft_y, soft_z, att_core, out_x, out_h,
    swap_send, swap_recv,
    zb_send, zb_recv, za_send, za_recv,
    yb_send, yb_recv, yf_send, ya_send, ya_recv, yaf_send,
    peer_send, pc_recv, py_recv, pz_recv, sy_recv, sz_recv, ac_recv, ox_recv, oh_recv,
):
    seq = lax.axis_index("seq")
    tp = lax.axis_index("tp")
    z, y, k = seq // 8, (seq // 2) % NY, seq % 2
    x, zh = tp // 2, tp % 2
    chip = seq // 2
    other = 1 - k

    def at(dz=0, dy=0, core=None):
        return {
            "seq": (z + dz) * 8 + lax.rem(y + dy, NY) * 2 + (k if core is None else core),
            "tp": tp,
        }

    partner = at(core=other)
    up, down = at(dy=1), at(dy=3)

    def y_peer(d):
        return at(dy=d)

    def z_peer(d):
        return {"seq": lax.rem(z + d, NZ) * 8 + y * 2 + k, "tp": tp}

    def x_peer(d):
        return {"seq": seq, "tp": lax.rem(x + d, NX) * 2 + zh}

    h_peer = {"seq": seq, "tp": x * 2 + 1 - zh}

    def copy(src, dst, ssem, rsem, dev):
        return pltpu.make_async_remote_copy(
            src_ref=src, dst_ref=dst, send_sem=ssem, recv_sem=rsem, device_id=dev, device_id_type=MESH
        )

    barrier = pltpu.get_barrier_semaphore()
    peers = [partner, h_peer]
    for d in (1, 2, 3):
        peers += [y_peer(d), z_peer(d), x_peer(d)]
    for dev in peers:
        pl.semaphore_signal(barrier, inc=1, device_id=dev, device_id_type=MESH)
    pl.semaphore_wait(barrier, len(peers))

    swap_kv = copy(
        kv_ref.at[other],
        blocks.at[z, y, pl.ds(pl.multiple_of(k * ROWS, ROWS), ROWS)],
        swap_send.at[0], swap_recv.at[0], partner,
    )
    swap_q = copy(q_ref.at[other], q_in, swap_send.at[1], swap_recv.at[1], partner)
    swap_kv.start()
    swap_q.start()
    blocks[z, y, pl.ds(pl.multiple_of(k * ROWS, ROWS), ROWS), :] = kv_ref[k]

    hid = hid_ref[...].astype(F32)
    squares = jnp.sum(hid * hid, axis=-1, keepdims=True)
    scaled_in = (hid * gain_ref[...]).astype(BF16)
    part = jnp.dot(scaled_in, wqkv_ref[...], preferred_element_type=F32)
    proj_core[k] = jnp.concatenate([part, jnp.broadcast_to(squares, (8, HD))], axis=1)
    core_send = copy(proj_core.at[k], proj_core.at[k], peer_send.at[0], pc_recv.at[k], partner)
    core_send.start()

    def spread(buf, peer, mine, n_peers, sends, first, recv):
        for d in range(1, n_peers + 1):
            copy(buf.at[mine], buf.at[mine], sends.at[first + d - 1], recv.at[mine], peer(d)).start()

    def gathered(buf, peer, mine, n_peers, sends, first, recv):
        for d in range(1, n_peers + 1):
            src = lax.rem(mine + d, n_peers + 1)
            c = copy(buf.at[src], buf.at[src], sends.at[first + d - 1], recv.at[src], peer(d))
            c.wait()

    def scale_queries(ref_rows, r):
        c = math.log2(math.e) / math.sqrt(HD)
        for h in range(HEADS):
            wide = ref_rows(h).astype(F32) * c
            top = wide.astype(BF16)
            q_scaled[2 * h + r] = jnp.concatenate([top, (wide - top.astype(F32)).astype(BF16)], axis=1)

    scale_queries(lambda h: q_ref[k, :, h * HD : (h + 1) * HD], 0)
    acc[...] = jnp.zeros_like(acc)
    tops[...] = jnp.full_like(tops, NEG)
    length = lens_ref[k]

    def attend(load, n, key_pos, causal):
        ones = jnp.ones((n, HD), BF16)
        bias = jnp.where(key_pos < length, 0.0, NEG)
        if causal:
            shape = (ROWS, n)
            row = lax.broadcasted_iota(jnp.int32, shape, 0)
            col = lax.broadcasted_iota(jnp.int32, shape, 1)

        @pl.loop(0, HEADS)
        def _(h):
            keys, values = load()
            keys = jnp.concatenate([keys, keys], axis=1)
            values = jnp.concatenate([values, ones], axis=1)
            for r in (0, 1):
                i = 2 * h + r
                s = lax.dot_general(q_scaled[i], keys, NT, preferred_element_type=F32)
                if causal:
                    s = jnp.where(col <= row + (k if r == 0 else other) * ROWS, s + bias, NEG)
                else:
                    s = s + bias
                before = tops[i]
                now = jnp.maximum(before, jnp.max(s, axis=-1, keepdims=True))
                p = jnp.exp2(s - jnp.concatenate([now] * (n // HD), axis=1))
                shrink = jnp.exp2(before - now)
                o = jnp.dot(p.astype(BF16), values, preferred_element_type=F32)
                acc[i] = acc[i] * jnp.concatenate([shrink, shrink], axis=1) + o
                tops[i] = now

    def positions(n):
        return lax.broadcasted_iota(jnp.int32, (1, n), 1)

    def whole_block(yp):
        def load():
            return blocks[z, yp, :, 0:HD], blocks[z, yp, :, HD : 2 * HD]

        return load

    def part_b(zp, yp):
        def load():
            at_b = blocks.at[zp, yp]
            return at_b[PART_A:BLOCK, 0:HD], at_b[PART_A:BLOCK, HD : 2 * HD]

        attend(load, PART_B, (zp * NY + yp) * BLOCK + PART_A + positions(PART_B), False)

    def part_a(zp):
        def load():
            rows = [blocks[zp, yp, 0:PART_A, :] for yp in range(NY)]
            rows = jnp.concatenate(rows, axis=0)
            return rows[:, 0:HD], rows[:, HD : 2 * HD]

        pos = positions(NY * PART_A)
        attend(load, NY * PART_A, zp * NY * BLOCK + (pos // PART_A) * BLOCK + pos % PART_A, False)

    a_rows = pl.ds(0, PART_A)
    b_rows = pl.ds(PART_A, PART_B)
    a_half = [pl.ds(0, HALF_A), pl.ds(HALF_A, HALF_A)]
    b_half = [pl.ds(PART_A, HALF_B), pl.ds(PART_A + HALF_B, HALF_B)]

    def moved(zp, yp, rows, ssem, rsem, dev):
        return copy(blocks.at[zp, yp, rows], blocks.at[zp, yp, rows], ssem, rsem, dev)

    def zb(zp):
        return moved(zp, y, b_rows, zb_send.at[zp], zb_recv.at[zp], z_peer(1))

    def za(zp, yp):
        return moved(zp, yp, a_rows, za_send.at[zp, yp], za_recv.at[zp, yp], z_peer(1))

    def yb(zp, direction, half, yp=None):
        return moved(
            zp, y if yp is None else yp, b_half[half],
            yb_send.at[zp, direction, half], yb_recv.at[zp, direction, half], (up, down)[direction],
        )

    def yb_forward(zp, direction):
        yp = lax.rem(y + (3, 1)[direction], NY)
        return moved(
            zp, yp, b_half[direction],
            yf_send.at[zp, direction], yb_recv.at[zp, 2, direction], (up, down)[direction],
        )

    def ya(direction, half, yp=None):
        return moved(
            z, y if yp is None else yp, a_half[half],
            ya_send.at[direction, half], ya_recv.at[direction, half], (up, down)[direction],
        )

    def ya_forward(direction):
        yp = lax.rem(y + (3, 1)[direction], NY)
        return moved(
            z, yp, a_half[direction],
            yaf_send.at[direction], ya_recv.at[2, direction], (up, down)[direction],
        )

    y_minus, y_plus, y_far = lax.rem(y + 3, NY), lax.rem(y + 1, NY), lax.rem(y + 2, NY)

    def send_b(zp):
        @pl.when(z < NZ - 1)
        def _():
            zb(zp).start()

        yb(zp, 0, 0).start()
        yb(zp, 1, 1).start()
        yb(zp, 0, 1).start()
        yb(zp, 1, 0).start()

    def forward_b(zp):
        yb(zp, 0, 0, y_minus).wait_recv()
        yb_forward(zp, 0).start()
        yb(zp, 1, 1, y_plus).wait_recv()
        yb_forward(zp, 1).start()

    def far_b(zp):
        for half in (0, 1):
            moved(zp, y_far, b_half[half], yf_send.at[zp, half], yb_recv.at[zp, 2, half], up).wait_recv()

    copy(
        kv_ref.at[k],
        blocks.at[z, y, pl.ds(pl.multiple_of(other * ROWS, ROWS), ROWS)],
        swap_send.at[0], swap_recv.at[0], partner,
    ).wait_recv()
    send_b(z)
    for half in (0, 1):
        ya(0, half).start()
        ya(1, 1 - half).start()

    @pl.when(z < NZ - 1)
    def _():
        za(z, y).start()

    copy(proj_core.at[other], proj_core.at[other], peer_send.at[0], pc_recv.at[other], partner).wait()
    proj_y[y] = proj_core[0] + proj_core[1]
    spread(proj_y, y_peer, y, 3, peer_send, 1, py_recv)

    swap_q.wait_recv()
    scale_queries(lambda h: q_in[:, h * HD : (h + 1) * HD], 1)
    attend(whole_block(y), BLOCK, chip * BLOCK + positions(BLOCK), True)

    gathered(proj_y, y_peer, y, 3, peer_send, 1, py_recv)
    proj_z[z] = (proj_y[0] + proj_y[1]) + (proj_y[2] + proj_y[3])
    spread(proj_z, z_peer, z, 3, peer_send, 4, pz_recv)

    forward_b(z)
    ya(0, 0, y_minus).wait_recv()
    ya_forward(0).start()
    ya(1, 1, y_plus).wait_recv()
    ya_forward(1).start()
    ya(0, 1, y_minus).wait_recv()
    ya(1, 0, y_plus).wait_recv()

    def next_b(j):
        @pl.when(j <= z)
        def _():
            zb(z - j).wait_recv()
            send_b(z - j)

    @pl.when(z < NZ - 1)
    def _():
        za(z, y_minus).start()
        za(z, y_plus).start()

    next_b(1)
    yb(z, 0, 1, y_minus).wait_recv()
    yb(z, 1, 0, y_plus).wait_recv()
    for half in (0, 1):
        moved(z, y_far, a_half[half], yaf_send.at[half], ya_recv.at[2, half], up).wait_recv()

    @pl.when(z < NZ - 1)
    def _():
        za(z, y_far).start()

    gathered(proj_z, z_peer, z, 3, peer_send, 4, pz_recv)
    total = (proj_z[0] + proj_z[1]) + (proj_z[2] + proj_z[3])
    proj = total[:, : 6 * HD] * lax.rsqrt(total[:, 6 * HD :][:, :1] / width + EPS)
    cosine, sine = cos_ref[...], sin_ref[...]

    def rotated(v):
        return (v * cosine + pltpu.roll(v, HD // 2, 1) * sine).astype(BF16)

    queries = jnp.concatenate([rotated(proj[:, h * HD : (h + 1) * HD]) for h in range(HEADS)], axis=0)
    blank = jnp.zeros((HD - 8, HD), F32)
    new_key = jnp.concatenate([rotated(proj[:, 4 * HD : 5 * HD]).astype(F32), blank], axis=0).astype(BF16)
    new_value = jnp.concatenate([proj[:, 5 * HD : 6 * HD], blank], axis=0).astype(BF16)
    own = blocks[z, y]
    keys = jnp.concatenate([own[:, :HD], new_key], axis=0)
    values = jnp.concatenate([own[:, HD:], new_value], axis=0)
    s = lax.dot_general(queries, keys, NT, preferred_element_type=F32) * (1.0 / math.sqrt(HD))
    row = lax.broadcasted_iota(jnp.int32, s.shape, 0) % 8
    col = lax.broadcasted_iota(jnp.int32, s.shape, 1)
    new = col - BLOCK
    old_ok = (col < BLOCK) & (chip * BLOCK + col < length)
    new_ok = (new >= 0) & (new <= row) & (new % 2 == row % 2) & (chip == 0)
    s = jnp.where(old_ok | new_ok, s, NEG)
    top = jnp.max(s, axis=-1, keepdims=True)
    p = jnp.exp(s - top)
    soft_y[y, 0] = jnp.dot(p.astype(BF16), values, preferred_element_type=F32)
    lane = lax.broadcasted_iota(jnp.int32, (32, HD), 1)

    def packed(top, sums):
        return jnp.where(lane < HD // 2, top, sums)

    soft_y[y, 1] = packed(top, jnp.sum(p, axis=-1, keepdims=True))
    spread(soft_y, y_peer, y, 3, peer_send, 7, sy_recv)

    def merge(buf):
        m = [buf[i, 1][:, :1] for i in range(4)]
        l = [buf[i, 1][:, HD - 1 :] for i in range(4)]
        top = jnp.maximum(jnp.maximum(m[0], m[1]), jnp.maximum(m[2], m[3]))
        w = [jnp.exp(t - top) for t in m]
        sums = (l[0] * w[0] + l[1] * w[1]) + (l[2] * w[2] + l[3] * w[3])
        o = (buf[0, 0] * w[0] + buf[1, 0] * w[1]) + (buf[2, 0] * w[2] + buf[3, 0] * w[3])
        return top, sums, o

    def decode_1():
        gathered(soft_y, y_peer, y, 3, peer_send, 7, sy_recv)
        top, sums, o = merge(soft_y)
        soft_z[z, 0] = o
        soft_z[z, 1] = packed(top, sums)
        spread(soft_z, z_peer, z, 3, peer_send, 10, sz_recv)

    def decode_2():
        gathered(soft_z, z_peer, z, 3, peer_send, 10, sz_recv)
        _, sums, o = merge(soft_z)
        att_core[k] = (o / sums).astype(BF16)
        copy(att_core.at[k], att_core.at[k], peer_send.at[13], ac_recv.at[k], partner).start()

    def decode_3():
        copy(att_core.at[other], att_core.at[other], peer_send.at[13], ac_recv.at[other], partner).wait()
        of_first = lax.broadcasted_iota(jnp.int32, (32, HD), 0) % 2 == 0
        att = jnp.where(of_first, att_core[0].astype(F32), att_core[1].astype(F32))
        out = jnp.zeros((8, ROWS), F32)
        for h in range(HEADS):
            out += jnp.dot(
                att[8 * h : 8 * h + 8].astype(BF16), wout_ref[h * HD : (h + 1) * HD, :],
                preferred_element_type=F32,
            )
        out_x[x] = out
        spread(out_x, x_peer, x, 3, peer_send, 14, ox_recv)

    def decode_4():
        gathered(out_x, x_peer, x, 3, peer_send, 14, ox_recv)
        out_h[zh] = (out_x[0] + out_x[1]) + (out_x[2] + out_x[3])
        copy(out_h.at[zh], out_h.at[zh], peer_send.at[17], oh_recv.at[zh], h_peer).start()

    def decode_5():
        copy(out_h.at[1 - zh], out_h.at[1 - zh], peer_send.at[17], oh_recv.at[1 - zh], h_peer).wait()
        dec_ref[...] = (hid_ref[...].astype(F32) + (out_h[0] + out_h[1])).astype(BF16)

    @pl.loop(1, 4)
    def _(d):
        yp = lax.rem(y + jnp.where(d == 1, 3, jnp.where(d == 2, 1, 2)), NY)

        @pl.when(d == 3)
        def _():
            far_b(z)

        @pl.when(yp < y)
        def _():
            attend(whole_block(yp), BLOCK, (z * NY + yp) * BLOCK + positions(BLOCK), False)

    decode_1()

    @pl.loop(1, NZ)
    def _(j):
        @pl.when(j <= z)
        def _():
            zp = z - j
            part_b(zp, y)
            forward_b(zp)
            next_b(j + 1)

            @pl.loop(1, 4)
            def _(d):
                yp = lax.rem(y + jnp.where(d == 1, 3, jnp.where(d == 2, 1, 2)), NY)

                @pl.when(d == 1)
                def _():
                    yb(zp, 0, 1, y_minus).wait_recv()

                @pl.when(d == 2)
                def _():
                    yb(zp, 1, 0, y_plus).wait_recv()

                @pl.when(d == 3)
                def _():
                    far_b(zp)

                part_b(zp, yp)

            for yp in range(NY):
                za(zp, yp).wait_recv()

            @pl.when(z < NZ - 1)
            def _():
                for yp in range(NY):
                    za(zp, yp).start()

            part_a(zp)

        @pl.when(j == 1)
        def _():
            decode_2()

        @pl.when(j == 2)
        def _():
            decode_3()

        @pl.when(j == 3)
        def _():
            decode_4()

    def result(i):
        return (acc[i][:, :HD] / acc[i][:, HD:]).astype(BF16)

    for h in range(HEADS):
        o_out[:, h * HD : (h + 1) * HD] = result(2 * h + 1)
    back = copy(o_out, o_in, swap_send.at[2], swap_recv.at[2], partner)
    back.start()
    for h in range(HEADS):
        attn_ref[k, :, h * HD : (h + 1) * HD] = result(2 * h)
    decode_5()

    swap_kv.wait_send()
    swap_q.wait_send()

    @pl.when(z < NZ - 1)
    def _():
        @pl.loop(0, NZ)
        def _(zp):
            @pl.when(zp <= z)
            def _():
                zb(zp).wait_send()
                for yp in range(NY):
                    za(zp, yp).wait_send()

    @pl.loop(0, NZ)
    def _(zp):
        @pl.when(zp <= z)
        def _():
            for direction in (0, 1):
                for half in (0, 1):
                    yb(zp, direction, half).wait_send()
                yb_forward(zp, direction).wait_send()

    for direction in (0, 1):
        for half in (0, 1):
            ya(direction, half).wait_send()
        ya_forward(direction).wait_send()
    back.wait()
    attn_ref[other] = o_in[...]


def on_device(q_prefill, kv_prefill, prompt_len, group_of, hidden, norm_gain, w_qkv, w_out):
    n_prompts, rows = q_prefill.shape[:2]
    cycle = lax.axis_size("seq")
    group_size = cycle // n_prompts
    piece = rows // group_size
    prompt_ids = jnp.arange(n_prompts, dtype=jnp.int32)
    prompt_of_group = jnp.sum(
        jnp.where(group_of[None, :] == prompt_ids[:, None], prompt_ids[None, :], 0), axis=1
    )
    chosen = jnp.take(kv_prefill, prompt_of_group, axis=0)
    outgoing = chosen.reshape(n_prompts * group_size, piece, 1, 2 * HD)
    cache_pages = lax.all_to_all(outgoing, "seq", split_axis=0, concat_axis=0, tiled=True)
    cache_pages = cache_pages.reshape(cycle * piece, 1, 2 * HD)

    steps = hidden.shape[0]
    half = HD // 2
    frequency = BASE ** (-2.0 * jnp.arange(half, dtype=F32) / HD)
    position = (prompt_len[None, :] + jnp.arange(steps, dtype=jnp.int32)[:, None]).reshape(-1)
    angle = position.astype(F32)[:, None] * frequency
    cosine, sine = jnp.cos(angle), jnp.sin(angle)
    cosine = jnp.concatenate([cosine, cosine], axis=1)
    sine = jnp.concatenate([-sine, sine], axis=1)

    vmem = pl.BlockSpec(memory_space=pltpu.VMEM)
    dma = pltpu.SemaphoreType.DMA
    width = hidden.shape[2] * cycle
    attn, decoded = pl.pallas_call(
        functools.partial(kernel, float(width)),
        out_shape=(
            jax.ShapeDtypeStruct((n_prompts, rows, HEADS * HD), BF16),
            jax.ShapeDtypeStruct((steps * n_prompts, rows), BF16),
        ),
        in_specs=[pl.BlockSpec(memory_space=pltpu.SMEM)] + [vmem] * 8,
        out_specs=(vmem, vmem),
        scratch_shapes=[
            pltpu.VMEM((NZ, NY, BLOCK, 2 * HD), BF16),
            pltpu.VMEM((ROWS, HEADS * HD), BF16),
            pltpu.VMEM((2 * HEADS, ROWS, 2 * HD), BF16),
            pltpu.VMEM((2 * HEADS, ROWS, 2 * HD), F32),
            pltpu.VMEM((2 * HEADS, ROWS, HD), F32),
            pltpu.VMEM((ROWS, HEADS * HD), BF16),
            pltpu.VMEM((ROWS, HEADS * HD), BF16),
            pltpu.VMEM((2, 8, 7 * HD), F32),
            pltpu.VMEM((NY, 8, 7 * HD), F32),
            pltpu.VMEM((NZ, 8, 7 * HD), F32),
            pltpu.VMEM((NY, 2, 32, HD), F32),
            pltpu.VMEM((NZ, 2, 32, HD), F32),
            pltpu.VMEM((2, 32, HD), BF16),
            pltpu.VMEM((NX, 8, ROWS), F32),
            pltpu.VMEM((2, 8, ROWS), F32),
            dma((3,)), dma((3,)),
            dma((NZ,)), dma((NZ,)), dma((NZ, NY)), dma((NZ, NY)),
            dma((NZ, 2, 2)), dma((NZ, 3, 2)), dma((NZ, 2)), dma((2, 2)), dma((3, 2)), dma((2,)),
            dma((18,)), dma((2,)), dma((NY,)), dma((NZ,)), dma((NY,)), dma((NZ,)), dma((2,)), dma((NX,)), dma((2,)),
        ],
        compiler_params=pltpu.CompilerParams(
            collective_id=0, has_side_effects=True, vmem_limit_bytes=40 * 1024 * 1024
        ),
        cost_estimate=pl.CostEstimate(flops=9 * 10**9, bytes_accessed=3 * 10**6, transcendentals=17 * 10**6),
    )(
        prompt_len,
        q_prefill.reshape(n_prompts, rows, HEADS * HD),
        kv_prefill.reshape(n_prompts, rows, 2 * HD),
        hidden.reshape(steps * n_prompts, rows),
        norm_gain.reshape(1, rows),
        w_qkv.reshape(rows, 6 * HD),
        w_out.reshape(HEADS * HD, rows),
        cosine,
        sine,
    )
    return (
        attn.reshape(n_prompts, rows, 1, HEADS * HD),
        cache_pages,
        decoded.reshape(steps, n_prompts, rows),
    )


def solution(mesh):
    placed = (
        P(None, "seq", "tp", None),
        P(None, "seq", "tp", None),
        P(),
        P(),
        P(None, None, "seq"),
        P("seq"),
        P("seq", "tp", None),
        P("tp", None, "seq"),
    )
    return jax.shard_map(
        on_device,
        mesh=mesh,
        in_specs=placed,
        out_specs=(P(None, "seq", "tp", None), P("seq", "tp", None), P(None, None, "seq")),
        check_vma=False,
    )
```

```python
import functools
import math

import jax
import jax.numpy as jnp
from jax import lax
from jax.experimental import pallas as pl
from jax.experimental.pallas import tpu as pltpu
from jax.sharding import PartitionSpec as P

MESH = pl.DeviceIdType.MESH
NEG = -1e30
EPS = 1e-05
BASE = 500000.0
ROWS = 256
BLOCK = 512
HD = 128
HEADS = 4
PART_A = 128
PART_B = BLOCK - PART_A
HALF_A, HALF_B = PART_A // 2, PART_B // 2
NY = 4
N_SEQ = 32
PIECE = 16
NZ = 4
NX = 4
BF16 = jnp.bfloat16
F32 = jnp.float32
NT = (((1,), (1,)), ((), ()))


def kernel(
    width,
    lens_ref, group_ref, q_ref, kv_ref, hid_ref, gain_ref, wqkv_ref, wout_ref, cos_ref, sin_ref,
    attn_ref, pages_ref, dec_ref,
    blocks, q_in, q_scaled, acc, tops, o_in, o_out,
    proj_core, proj_y, proj_z, soft_y, soft_z, att_core, out_x, out_h, by_group, pages,
    swap_send, swap_recv,
    zb_send, zb_recv, za_send, za_recv,
    yb_send, yb_recv, yf_send, ya_send, ya_recv, yaf_send,
    peer_send, pc_recv, py_recv, pz_recv, sy_recv, sz_recv, ac_recv, ox_recv, oh_recv,
    page_send, page_recv, page_own,
):
    seq = lax.axis_index("seq")
    tp = lax.axis_index("tp")
    z, y, k = seq // 8, (seq // 2) % NY, seq % 2
    x, zh = tp // 2, tp % 2
    chip = seq // 2
    other = 1 - k

    def at(dz=0, dy=0, core=None):
        return {
            "seq": (z + dz) * 8 + lax.rem(y + dy, NY) * 2 + (k if core is None else core),
            "tp": tp,
        }

    partner = at(core=other)
    up, down = at(dy=1), at(dy=3)

    def y_peer(d):
        return at(dy=d)

    def z_peer(d):
        return {"seq": lax.rem(z + d, NZ) * 8 + y * 2 + k, "tp": tp}

    def x_peer(d):
        return {"seq": seq, "tp": lax.rem(x + d, NX) * 2 + zh}

    h_peer = {"seq": seq, "tp": x * 2 + 1 - zh}

    def copy(src, dst, ssem, rsem, dev):
        return pltpu.make_async_remote_copy(
            src_ref=src, dst_ref=dst, send_sem=ssem, recv_sem=rsem, device_id=dev, device_id_type=MESH
        )

    barrier = pltpu.get_barrier_semaphore()
    peers = [h_peer, x_peer(1), x_peer(2), x_peer(3)]
    for dev in peers:
        pl.semaphore_signal(barrier, inc=1, device_id=dev, device_id_type=MESH)

    @pl.loop(1, N_SEQ)
    def _(d):
        dev = {"seq": lax.rem(seq + d, N_SEQ), "tp": tp}
        pl.semaphore_signal(barrier, inc=1, device_id=dev, device_id_type=MESH)

    second = (group_ref[0] != 0).astype(jnp.int32)
    by_group[0] = kv_ref[second].reshape(N_SEQ // 2, PIECE, 2 * HD)
    by_group[1] = kv_ref[1 - second].reshape(N_SEQ // 2, PIECE, 2 * HD)

    def page(owner, source):
        dev = {"seq": owner, "tp": tp}
        return copy(
            by_group.at[owner // 16, lax.rem(owner, 16)], pages.at[source],
            page_send.at[owner], page_recv.at[source], dev,
        )

    hid = hid_ref[...].astype(F32)
    squares = jnp.sum(hid * hid, axis=-1, keepdims=True)
    scaled_in = (hid * gain_ref[...]).astype(BF16)
    part = jnp.dot(scaled_in, wqkv_ref[...], preferred_element_type=F32)
    proj_core[k] = jnp.concatenate([part, jnp.broadcast_to(squares, (8, HD))], axis=1)
    blocks[z, y, pl.ds(pl.multiple_of(k * ROWS, ROWS), ROWS), :] = kv_ref[k]

    pl.semaphore_wait(barrier, len(peers) + N_SEQ - 1)

    swap_kv = copy(
        kv_ref.at[other],
        blocks.at[z, y, pl.ds(pl.multiple_of(k * ROWS, ROWS), ROWS)],
        swap_send.at[0], swap_recv.at[0], partner,
    )
    swap_q = copy(q_ref.at[other], q_in, swap_send.at[1], swap_recv.at[1], partner)
    swap_kv.start()
    swap_q.start()
    core_send = copy(proj_core.at[k], proj_core.at[k], peer_send.at[0], pc_recv.at[k], partner)
    core_send.start()

    @pl.loop(1, N_SEQ)
    def _(d):
        page(lax.rem(seq + d, N_SEQ), seq).start()

    own_page = pltpu.make_async_copy(by_group.at[seq // 16, lax.rem(seq, 16)], pages.at[seq], page_own)
    own_page.start()

    def spread(buf, peer, mine, n_peers, sends, first, recv):
        for d in range(1, n_peers + 1):
            copy(buf.at[mine], buf.at[mine], sends.at[first + d - 1], recv.at[mine], peer(d)).start()

    def gathered(buf, peer, mine, n_peers, sends, first, recv):
        for d in range(1, n_peers + 1):
            src = lax.rem(mine + d, n_peers + 1)
            c = copy(buf.at[src], buf.at[src], sends.at[first + d - 1], recv.at[src], peer(d))
            c.wait()

    def scale_queries(ref_rows, r):
        c = math.log2(math.e) / math.sqrt(HD)
        for h in range(HEADS):
            wide = ref_rows(h).astype(F32) * c
            top = wide.astype(BF16)
            q_scaled[2 * h + r] = jnp.concatenate([top, (wide - top.astype(F32)).astype(BF16)], axis=1)

    scale_queries(lambda h: q_ref[k, :, h * HD : (h + 1) * HD], 0)
    acc[...] = jnp.zeros_like(acc)
    tops[...] = jnp.full_like(tops, NEG)
    length = lens_ref[k]

    def attend(keys, values, key_pos, causal=False):
        n = keys.shape[0]
        bias = jnp.where(key_pos < length, 0.0, NEG)
        keys = jnp.concatenate([keys, keys], axis=1)
        values = jnp.concatenate([values, jnp.ones((n, HD), BF16)], axis=1)
        if causal:
            row = lax.broadcasted_iota(jnp.int32, (ROWS, n), 0)
            col = lax.broadcasted_iota(jnp.int32, (ROWS, n), 1)
            seen = [jnp.where(col <= row + core * ROWS, bias, NEG) for core in (k, other)]

        def scores(i):
            s = lax.dot_general(q_scaled[i], keys, NT, preferred_element_type=F32)
            return s + (seen[i % 2] if causal else bias)

        s = scores(0)
        for i in range(2 * HEADS):
            ahead = scores(i + 1) if i + 1 < 2 * HEADS else None
            before = tops[i]
            now = jnp.maximum(before, jnp.max(s, axis=-1, keepdims=True))
            p = jnp.exp2(s - jnp.concatenate([now] * (n // HD), axis=1)).astype(BF16)
            shrink = jnp.exp2(before - now)
            tops[i] = now
            o = jnp.dot(p, values, preferred_element_type=F32)
            acc[i] = acc[i] * jnp.concatenate([shrink, shrink], axis=1) + o
            s = ahead

    def positions(n):
        return lax.broadcasted_iota(jnp.int32, (1, n), 1)

    def whole_block(yp, causal=False):
        rows = blocks[z, yp]
        attend(rows[:, :HD], rows[:, HD:], (z * NY + yp) * BLOCK + positions(BLOCK), causal)

    def parts(zp, in_b, with_a):
        rows = [blocks[zp, yp, PART_A:BLOCK, :] for yp in in_b]
        pos = [(zp * NY + yp) * BLOCK + PART_A + positions(PART_B) for yp in in_b]
        if with_a:
            rows += [blocks[zp, yp, 0:PART_A, :] for yp in range(NY)]
            pos += [(zp * NY + yp) * BLOCK + positions(PART_A) for yp in range(NY)]
        rows = jnp.concatenate(rows, axis=0)
        attend(rows[:, :HD], rows[:, HD:], jnp.concatenate(pos, axis=1))

    a_rows = pl.ds(0, PART_A)
    b_rows = pl.ds(PART_A, PART_B)
    a_half = [pl.ds(0, HALF_A), pl.ds(HALF_A, HALF_A)]
    b_half = [pl.ds(PART_A, HALF_B), pl.ds(PART_A + HALF_B, HALF_B)]

    def moved(zp, yp, rows, ssem, rsem, dev):
        return copy(blocks.at[zp, yp, rows], blocks.at[zp, yp, rows], ssem, rsem, dev)

    def zb(zp):
        return moved(zp, y, b_rows, zb_send.at[zp], zb_recv.at[zp], z_peer(1))

    def za(zp, yp):
        return moved(zp, yp, a_rows, za_send.at[zp, yp], za_recv.at[zp, yp], z_peer(1))

    def yb(zp, direction, half, yp=None):
        return moved(
            zp, y if yp is None else yp, b_half[half],
            yb_send.at[zp, direction, half], yb_recv.at[zp, direction, half], (up, down)[direction],
        )

    def yb_forward(zp, direction):
        yp = lax.rem(y + (3, 1)[direction], NY)
        return moved(
            zp, yp, b_half[direction],
            yf_send.at[zp, direction], yb_recv.at[zp, 2, direction], (up, down)[direction],
        )

    def ya(direction, half, yp=None):
        return moved(
            z, y if yp is None else yp, a_half[half],
            ya_send.at[direction, half], ya_recv.at[direction, half], (up, down)[direction],
        )

    def ya_forward(direction):
        yp = lax.rem(y + (3, 1)[direction], NY)
        return moved(
            z, yp, a_half[direction],
            yaf_send.at[direction], ya_recv.at[2, direction], (up, down)[direction],
        )

    y_minus, y_plus, y_far = lax.rem(y + 3, NY), lax.rem(y + 1, NY), lax.rem(y + 2, NY)

    def send_b(zp):
        @pl.when(z < NZ - 1)
        def _():
            zb(zp).start()

        yb(zp, 0, 0).start()
        yb(zp, 1, 1).start()
        yb(zp, 0, 1).start()
        yb(zp, 1, 0).start()

    def forward_b(zp):
        yb(zp, 0, 0, y_minus).wait_recv()
        yb_forward(zp, 0).start()
        yb(zp, 1, 1, y_plus).wait_recv()
        yb_forward(zp, 1).start()

    def far_b(zp):
        for half in (0, 1):
            moved(zp, y_far, b_half[half], yf_send.at[zp, half], yb_recv.at[zp, 2, half], up).wait_recv()

    copy(
        kv_ref.at[k],
        blocks.at[z, y, pl.ds(pl.multiple_of(other * ROWS, ROWS), ROWS)],
        swap_send.at[0], swap_recv.at[0], partner,
    ).wait_recv()
    send_b(z)
    for half in (0, 1):
        ya(0, half).start()
        ya(1, 1 - half).start()

    @pl.when(z < NZ - 1)
    def _():
        za(z, y).start()

    copy(proj_core.at[other], proj_core.at[other], peer_send.at[0], pc_recv.at[other], partner).wait()
    proj_y[y] = proj_core[0] + proj_core[1]
    spread(proj_y, y_peer, y, 3, peer_send, 1, py_recv)

    swap_q.wait_recv()
    scale_queries(lambda h: q_in[:, h * HD : (h + 1) * HD], 1)
    whole_block(y, True)

    forward_b(z)
    ya(0, 0, y_minus).wait_recv()
    ya_forward(0).start()
    ya(1, 1, y_plus).wait_recv()
    ya_forward(1).start()
    ya(0, 1, y_minus).wait_recv()
    ya(1, 0, y_plus).wait_recv()

    def next_b(j):
        @pl.when(j <= z)
        def _():
            zb(z - j).wait_recv()
            send_b(z - j)

    @pl.when(z < NZ - 1)
    def _():
        za(z, y_minus).start()
        za(z, y_plus).start()

    next_b(1)
    yb(z, 0, 1, y_minus).wait_recv()
    yb(z, 1, 0, y_plus).wait_recv()
    for half in (0, 1):
        moved(z, y_far, a_half[half], yaf_send.at[half], ya_recv.at[2, half], up).wait_recv()

    @pl.when(z < NZ - 1)
    def _():
        za(z, y_far).start()

    lane = lax.broadcasted_iota(jnp.int32, (32, HD), 1)

    def packed(top, sums):
        return jnp.where(lane < HD // 2, top, sums)

    def decode_0():
        gathered(proj_y, y_peer, y, 3, peer_send, 1, py_recv)
        proj_z[z] = (proj_y[0] + proj_y[1]) + (proj_y[2] + proj_y[3])
        spread(proj_z, z_peer, z, 3, peer_send, 4, pz_recv)

    def decode_1():
        gathered(proj_z, z_peer, z, 3, peer_send, 4, pz_recv)
        total = (proj_z[0] + proj_z[1]) + (proj_z[2] + proj_z[3])
        proj = total[:, : 6 * HD] * lax.rsqrt(total[:, 6 * HD :][:, :1] / width + EPS)
        cosine, sine = cos_ref[...], sin_ref[...]

        def rotated(v):
            return (v * cosine + pltpu.roll(v, HD // 2, 1) * sine).astype(BF16)

        queries = jnp.concatenate([rotated(proj[:, h * HD : (h + 1) * HD]) for h in range(HEADS)], axis=0)
        blank = jnp.zeros((HD - 8, HD), F32)
        new_key = jnp.concatenate([rotated(proj[:, 4 * HD : 5 * HD]).astype(F32), blank], axis=0).astype(BF16)
        new_value = jnp.concatenate([proj[:, 5 * HD : 6 * HD], blank], axis=0).astype(BF16)
        own = blocks[z, y]
        keys = jnp.concatenate([own[:, :HD], new_key], axis=0)
        values = jnp.concatenate([own[:, HD:], new_value], axis=0)
        s = lax.dot_general(queries, keys, NT, preferred_element_type=F32) * (1.0 / math.sqrt(HD))
        row = lax.broadcasted_iota(jnp.int32, s.shape, 0) % 8
        col = lax.broadcasted_iota(jnp.int32, s.shape, 1)
        new = col - BLOCK
        old_ok = (col < BLOCK) & (chip * BLOCK + col < length)
        new_ok = (new >= 0) & (new <= row) & (new % 2 == row % 2) & (chip == 0)
        s = jnp.where(old_ok | new_ok, s, NEG)
        top = jnp.max(s, axis=-1, keepdims=True)
        p = jnp.exp(s - top)
        soft_y[y, 0] = jnp.dot(p.astype(BF16), values, preferred_element_type=F32)
        soft_y[y, 1] = packed(top, jnp.sum(p, axis=-1, keepdims=True))
        spread(soft_y, y_peer, y, 3, peer_send, 7, sy_recv)

    def merge(buf):
        m = [buf[i, 1][:, :1] for i in range(4)]
        l = [buf[i, 1][:, HD - 1 :] for i in range(4)]
        top = jnp.maximum(jnp.maximum(m[0], m[1]), jnp.maximum(m[2], m[3]))
        w = [jnp.exp(t - top) for t in m]
        sums = (l[0] * w[0] + l[1] * w[1]) + (l[2] * w[2] + l[3] * w[3])
        o = (buf[0, 0] * w[0] + buf[1, 0] * w[1]) + (buf[2, 0] * w[2] + buf[3, 0] * w[3])
        return top, sums, o

    def decode_2():
        gathered(soft_y, y_peer, y, 3, peer_send, 7, sy_recv)
        top, sums, o = merge(soft_y)
        soft_z[z, 0] = o
        soft_z[z, 1] = packed(top, sums)
        spread(soft_z, z_peer, z, 3, peer_send, 10, sz_recv)

    def decode_3():
        gathered(soft_z, z_peer, z, 3, peer_send, 10, sz_recv)
        _, sums, o = merge(soft_z)
        att_core[k] = (o / sums).astype(BF16)
        copy(att_core.at[k], att_core.at[k], peer_send.at[13], ac_recv.at[k], partner).start()

    def decode_4():
        copy(att_core.at[other], att_core.at[other], peer_send.at[13], ac_recv.at[other], partner).wait()
        of_first = lax.broadcasted_iota(jnp.int32, (32, HD), 0) % 2 == 0
        att = jnp.where(of_first, att_core[0].astype(F32), att_core[1].astype(F32))
        out = jnp.zeros((8, ROWS), F32)
        for h in range(HEADS):
            out += jnp.dot(
                att[8 * h : 8 * h + 8].astype(BF16), wout_ref[h * HD : (h + 1) * HD, :],
                preferred_element_type=F32,
            )
        out_x[x] = out
        spread(out_x, x_peer, x, 3, peer_send, 14, ox_recv)

    def decode_5():
        gathered(out_x, x_peer, x, 3, peer_send, 14, ox_recv)
        out_h[zh] = (out_x[0] + out_x[1]) + (out_x[2] + out_x[3])
        copy(out_h.at[zh], out_h.at[zh], peer_send.at[17], oh_recv.at[zh], h_peer).start()

    def decode_6():
        copy(out_h.at[1 - zh], out_h.at[1 - zh], peer_send.at[17], oh_recv.at[1 - zh], h_peer).wait()
        dec_ref[...] = (hid_ref[...].astype(F32) + (out_h[0] + out_h[1])).astype(BF16)

    @pl.loop(1, 4)
    def _(d):
        yp = lax.rem(y + jnp.where(d == 1, 3, jnp.where(d == 2, 1, 2)), NY)

        @pl.when(d == 3)
        def _():
            far_b(z)

        @pl.when(yp < y)
        def _():
            whole_block(yp)

        @pl.when(d == 1)
        def _():
            decode_0()

        @pl.when(d == 3)
        def _():
            decode_1()

    @pl.loop(1, NZ)
    def _(j):
        @pl.when(j <= z)
        def _():
            zp = z - j
            parts(zp, [y], False)
            forward_b(zp)
            next_b(j + 1)

        @pl.when(j == 1)
        def _():
            decode_2()

        @pl.when(j == 2)
        def _():
            decode_4()

        @pl.when(j == 3)
        def _():
            decode_6()

        @pl.when(j <= z)
        def _():
            zp = z - j
            yb(zp, 0, 1, y_minus).wait_recv()
            yb(zp, 1, 0, y_plus).wait_recv()
            parts(zp, [y_minus, y_plus], False)
            far_b(zp)
            for yp in range(NY):
                za(zp, yp).wait_recv()

            @pl.when(z < NZ - 1)
            def _():
                for yp in range(NY):
                    za(zp, yp).start()

            parts(zp, [y_far], True)

        @pl.when(j == 1)
        def _():
            decode_3()

        @pl.when(j == 2)
        def _():
            decode_5()

    def result(i):
        return (acc[i][:, :HD] / acc[i][:, HD:]).astype(BF16)

    for h in range(HEADS):
        o_out[:, h * HD : (h + 1) * HD] = result(2 * h + 1)
    back = copy(o_out, o_in, swap_send.at[2], swap_recv.at[2], partner)
    back.start()
    for h in range(HEADS):
        attn_ref[k, :, h * HD : (h + 1) * HD] = result(2 * h)

    swap_kv.wait_send()
    swap_q.wait_send()
    own_page.wait()

    @pl.loop(1, N_SEQ)
    def _(d):
        page(lax.rem(seq + d, N_SEQ), lax.rem(seq + d, N_SEQ)).wait()

    pages_ref[...] = pages[...].reshape(N_SEQ * PIECE, 2 * HD)

    @pl.when(z < NZ - 1)
    def _():
        @pl.loop(0, NZ)
        def _(zp):
            @pl.when(zp <= z)
            def _():
                zb(zp).wait_send()
                for yp in range(NY):
                    za(zp, yp).wait_send()

    @pl.loop(0, NZ)
    def _(zp):
        @pl.when(zp <= z)
        def _():
            for direction in (0, 1):
                for half in (0, 1):
                    yb(zp, direction, half).wait_send()
                yb_forward(zp, direction).wait_send()

    for direction in (0, 1):
        for half in (0, 1):
            ya(direction, half).wait_send()
        ya_forward(direction).wait_send()
    back.wait()
    attn_ref[other] = o_in[...]


def on_device(q_prefill, kv_prefill, prompt_len, group_of, hidden, norm_gain, w_qkv, w_out):
    n_prompts, rows = q_prefill.shape[:2]
    cycle = lax.axis_size("seq")

    steps = hidden.shape[0]
    half = HD // 2
    frequency = BASE ** (-2.0 * jnp.arange(half, dtype=F32) / HD)
    position = (prompt_len[None, :] + jnp.arange(steps, dtype=jnp.int32)[:, None]).reshape(-1)
    angle = position.astype(F32)[:, None] * frequency
    cosine, sine = jnp.cos(angle), jnp.sin(angle)
    cosine = jnp.concatenate([cosine, cosine], axis=1)
    sine = jnp.concatenate([-sine, sine], axis=1)

    vmem = pl.BlockSpec(memory_space=pltpu.VMEM)
    dma = pltpu.SemaphoreType.DMA
    width = hidden.shape[2] * cycle
    attn, pages, decoded = pl.pallas_call(
        functools.partial(kernel, float(width)),
        out_shape=(
            jax.ShapeDtypeStruct((n_prompts, rows, HEADS * HD), BF16),
            jax.ShapeDtypeStruct((N_SEQ * PIECE, 2 * HD), BF16),
            jax.ShapeDtypeStruct((steps * n_prompts, rows), BF16),
        ),
        in_specs=[pl.BlockSpec(memory_space=pltpu.SMEM)] * 2 + [vmem] * 8,
        out_specs=(vmem, vmem, vmem),
        scratch_shapes=[
            pltpu.VMEM((NZ, NY, BLOCK, 2 * HD), BF16),
            pltpu.VMEM((ROWS, HEADS * HD), BF16),
            pltpu.VMEM((2 * HEADS, ROWS, 2 * HD), BF16),
            pltpu.VMEM((2 * HEADS, ROWS, 2 * HD), F32),
            pltpu.VMEM((2 * HEADS, ROWS, HD), F32),
            pltpu.VMEM((ROWS, HEADS * HD), BF16),
            pltpu.VMEM((ROWS, HEADS * HD), BF16),
            pltpu.VMEM((2, 8, 7 * HD), F32),
            pltpu.VMEM((NY, 8, 7 * HD), F32),
            pltpu.VMEM((NZ, 8, 7 * HD), F32),
            pltpu.VMEM((NY, 2, 32, HD), F32),
            pltpu.VMEM((NZ, 2, 32, HD), F32),
            pltpu.VMEM((2, 32, HD), BF16),
            pltpu.VMEM((NX, 8, ROWS), F32),
            pltpu.VMEM((2, 8, ROWS), F32),
            pltpu.VMEM((2, N_SEQ // 2, PIECE, 2 * HD), BF16),
            pltpu.VMEM((N_SEQ, PIECE, 2 * HD), BF16),
            dma((3,)), dma((3,)),
            dma((NZ,)), dma((NZ,)), dma((NZ, NY)), dma((NZ, NY)),
            dma((NZ, 2, 2)), dma((NZ, 3, 2)), dma((NZ, 2)), dma((2, 2)), dma((3, 2)), dma((2,)),
            dma((18,)), dma((2,)), dma((NY,)), dma((NZ,)), dma((NY,)), dma((NZ,)), dma((2,)), dma((NX,)), dma((2,)),
            dma((N_SEQ,)), dma((N_SEQ,)), dma,
        ],
        compiler_params=pltpu.CompilerParams(
            collective_id=0, has_side_effects=True, vmem_limit_bytes=40 * 1024 * 1024
        ),
        cost_estimate=pl.CostEstimate(flops=9 * 10**9, bytes_accessed=3 * 10**6, transcendentals=17 * 10**6),
    )(
        prompt_len,
        group_of,
        q_prefill.reshape(n_prompts, rows, HEADS * HD),
        kv_prefill.reshape(n_prompts, rows, 2 * HD),
        hidden.reshape(steps * n_prompts, rows),
        norm_gain.reshape(1, rows),
        w_qkv.reshape(rows, 6 * HD),
        w_out.reshape(HEADS * HD, rows),
        cosine,
        sine,
    )
    return (
        attn.reshape(n_prompts, rows, 1, HEADS * HD),
        pages.reshape(N_SEQ * PIECE, 1, 2 * HD),
        decoded.reshape(steps, n_prompts, rows),
    )


def solution(mesh):
    placed = (
        P(None, "seq", "tp", None),
        P(None, "seq", "tp", None),
        P(),
        P(),
        P(None, None, "seq"),
        P("seq"),
        P("seq", "tp", None),
        P("tp", None, "seq"),
    )
    return jax.shard_map(
        on_device,
        mesh=mesh,
        in_specs=placed,
        out_specs=(P(None, "seq", "tp", None), P("seq", "tp", None), P(None, None, "seq")),
        check_vma=False,
    )
```

```python
import functools
import math

import jax
import jax.numpy as jnp
import numpy as np
from jax import lax
from jax.experimental import pallas as pl
from jax.experimental.pallas import tpu as pltpu
from jax.sharding import PartitionSpec as P

MESH = pl.DeviceIdType.MESH
NEG = -1e30
EPS = 1e-05
BASE = 500000.0
ROWS = 256
BLOCK = 512
HD = 128
HEADS = 4
NY = 4
NZ = 4
ROW = 8
N_TP = 8
EARLY = 1
N_SEQ = 32
PIECE = 16
BF16 = jnp.bfloat16
F32 = jnp.float32
NT = (((1,), (1,)), ((), ()))


def kernel(
    width,
    lens_ref, group_ref, q_ref, kv_ref, hid_ref, gain_ref, wqkv_ref, wout_ref, freq_ref,
    attn_ref, pages_ref, dec_ref,
    blocks, kv_own, q_own, q_in, wqkv, wout, q_scaled, acc, tops, o_in, o_out, o_own,
    proj_row, proj_z, soft_row, soft_z, out_tp, by_group, pages,
    local, swap_send, swap_recv, chunk_recv, chip_recv,
    first_send, forward_send, chip_send, far_send,
    peer_send, pr_recv, pz_recv, sr_recv, sz_recv, ot_recv,
    page_send, page_recv,
):
    seq = lax.axis_index("seq")
    tp = lax.axis_index("tp")
    z, y, k = seq // 8, (seq // 2) % NY, seq % 2
    big, s = z // 2, z % 2
    other = 1 - k

    def on(zz, yy, core):
        return {"seq": zz * 8 + yy * 2 + core, "tp": tp}

    mate = on(z, y, other)
    pair = on(big * 2 + 1 - s, y, k)
    up, down = on(z, lax.rem(y + 1, NY), k), on(z, lax.rem(y + 3, NY), k)

    def row_peer(d):
        place = lax.rem(2 * y + k + d, ROW)
        return on(z, place // 2, lax.rem(place, 2))

    def z_peer(d):
        return on(lax.rem(z + d, NZ), y, k)

    def tp_peer(d):
        return {"seq": seq, "tp": lax.rem(tp + d, N_TP)}

    def copy(src, dst, ssem, rsem, dev):
        return pltpu.make_async_remote_copy(
            src_ref=src, dst_ref=dst, send_sem=ssem, recv_sem=rsem, device_id=dev, device_id_type=MESH
        )

    loads = [
        pltpu.make_async_copy(src, dst, local.at[i])
        for i, (src, dst) in enumerate([
            (kv_ref, kv_own), (kv_ref.at[s], blocks.at[big, y, s, k]), (wqkv_ref, wqkv),
            (q_ref.at[s], q_own), (wout_ref, wout),
        ])
    ]
    for load in loads:
        load.start()

    barrier = pltpu.get_barrier_semaphore()

    @pl.loop(1, N_TP)
    def _(d):
        pl.semaphore_signal(barrier, inc=1, device_id=tp_peer(d), device_id_type=MESH)

    @pl.loop(1, N_SEQ)
    def _(d):
        dev = {"seq": lax.rem(seq + d, N_SEQ), "tp": tp}
        pl.semaphore_signal(barrier, inc=1, device_id=dev, device_id_type=MESH)

    acc[...] = jnp.zeros_like(acc)
    tops[...] = jnp.full_like(tops, NEG)

    loads[0].wait()
    second = (group_ref[0] != 0).astype(jnp.int32)
    by_group[0] = kv_own[second].reshape(N_SEQ // 2, PIECE, 2 * HD)
    by_group[1] = kv_own[1 - second].reshape(N_SEQ // 2, PIECE, 2 * HD)

    def page(owner, source):
        return copy(
            by_group.at[owner // 16, lax.rem(owner, 16)], pages.at[source],
            page_send.at[owner], page_recv.at[source], {"seq": owner, "tp": tp},
        )

    loads[2].wait()
    hid = jnp.concatenate([hid_ref[i].astype(F32) for i in range(hid_ref.shape[0])], axis=0)
    squares = jnp.sum(hid * hid, axis=-1, keepdims=True)
    scaled_in = (hid * gain_ref[...]).astype(BF16)
    part = jnp.dot(scaled_in, wqkv[...], preferred_element_type=F32)
    proj_row[2 * y + k] = jnp.concatenate([part, jnp.broadcast_to(squares, (8, HD))], axis=1)
    loads[1].wait()

    def chunk(zp, yp, zc, ssem, dev, to_mate=False):
        ref = blocks.at[zp, yp, zc, k]
        return copy(ref, ref, ssem, (chip_recv if to_mate else chunk_recv).at[zp, yp, zc], dev)

    def to_mate(zp, yp, zc):
        return chunk(zp, yp, zc, chip_send.at[zp, yp, zc], mate, True)

    def first(zp, direction, zc):
        return chunk(zp, y, zc, first_send.at[zp, direction, zc], (up, down)[direction])

    y_minus, y_plus, y_far = lax.rem(y + 3, NY), lax.rem(y + 1, NY), lax.rem(y + 2, NY)

    def forward(zp, direction):
        return chunk(zp, (y_minus, y_plus)[direction], direction, forward_send.at[zp, direction], (up, down)[direction])

    def far(prompt):
        return copy(
            kv_ref.at[prompt], blocks.at[0, y, s, k], far_send.at[prompt], chunk_recv.at[0, y, s], on(2 + prompt, y, k)
        )

    def arrived(zp, yp, zc):
        chunk(zp, yp, zc, chip_send.at[0, 0, 0], mate).wait_recv()

    def mate_arrived(zp, yp, zc):
        ref = blocks.at[zp, yp, zc, other]
        copy(ref, ref, chip_send.at[0, 0, 0], chip_recv.at[zp, yp, zc], mate).wait_recv()

    def hand_out(zp, zc):
        first(zp, 0, zc).start()
        first(zp, 1, zc).start()
        to_mate(zp, y, zc).start()

    def pass_on(zp, direction):
        yp = (y_minus, y_plus)[direction]
        arrived(zp, yp, direction)
        forward(zp, direction).start()
        to_mate(zp, yp, direction).start()

    def take(zp, yp, zc):
        arrived(zp, yp, zc)
        to_mate(zp, yp, zc).start()

    swap_kv = copy(
        kv_ref.at[1 - s], blocks.at[big, y, s, k], swap_send.at[0], chunk_recv.at[big, y, s], pair
    )
    swap_q = copy(q_ref.at[1 - s], q_in, swap_send.at[1], swap_recv.at[0], pair)

    pl.semaphore_wait(barrier, N_TP + N_SEQ - 2)

    swap_kv.start()
    hand_out(big, s)

    @pl.when(big == 0)
    def _():
        far(0).start()
        far(1).start()

    swap_q.start()
    own_page = pltpu.make_async_copy(by_group.at[seq // 16, lax.rem(seq, 16)], pages.at[seq], local.at[5])
    own_page.start()

    def spread(buf, peer, mine, n_peers, sends, first, recv):
        for d in range(1, n_peers + 1):
            copy(buf.at[mine], buf.at[mine], sends.at[first + d - 1], recv.at[mine], peer(d)).start()

    def gathered(buf, peer, mine, n_peers, sends, first, recv):
        for d in range(1, n_peers + 1):
            src = lax.rem(mine + d, n_peers + 1)
            c = copy(buf.at[src], buf.at[src], sends.at[first + d - 1], recv.at[src], peer(d))
            c.wait()

    spread(proj_row, row_peer, 2 * y + k, ROW - 1, peer_send, 0, pr_recv)

    def scale_queries(ref, r):
        c = math.log2(math.e) / math.sqrt(HD)
        for h in range(HEADS):
            wide = ref[:, h * HD : (h + 1) * HD].astype(F32) * c
            top = wide.astype(BF16)
            q_scaled[r, h] = jnp.concatenate([top, (wide - top.astype(F32)).astype(BF16)], axis=1)

    length = lens_ref[s]

    def attend(r, rows, bias):
        n = rows.shape[0]
        keys, values = rows[:, :HD], rows[:, HD:]
        keys = jnp.concatenate([keys, keys], axis=1)
        values = jnp.concatenate([values, jnp.ones((n, HD), BF16)], axis=1)

        def scores(h):
            return lax.dot_general(q_scaled[r, h], keys, NT, preferred_element_type=F32) + bias

        now_scores = scores(0)
        for h in range(HEADS):
            ahead = scores(h + 1) if h + 1 < HEADS else None
            before = tops[r, h]
            now = jnp.maximum(before, jnp.max(now_scores, axis=-1, keepdims=True))
            p = jnp.exp2(now_scores - jnp.concatenate([now] * (n // HD), axis=1)).astype(BF16)
            shrink = jnp.exp2(before - now)
            tops[r, h] = now
            o = jnp.dot(p, values, preferred_element_type=F32)
            acc[r, h] = acc[r, h] * jnp.concatenate([shrink, shrink], axis=1) + o
            now_scores = ahead

    def near_step(r, yp, zc):
        key_at = ((2 * big + zc) * NY + yp) * BLOCK
        row_at = ((2 * big + r) * NY + y) * BLOCK + k * ROWS
        row = row_at + lax.broadcasted_iota(jnp.int32, (ROWS, BLOCK), 0)
        col = key_at + lax.broadcasted_iota(jnp.int32, (ROWS, BLOCK), 1)
        bias = jnp.where(col < jnp.minimum(row + 1, length), 0.0, NEG)
        attend(r, blocks[big, yp, zc].reshape(BLOCK, 2 * HD), bias)

    def far_step(r, yp):
        attend(r, blocks[0, yp].reshape(2 * BLOCK, 2 * HD), 0.0)

    lane = lax.broadcasted_iota(jnp.int32, (32, HD), 1)

    def packed(top, sums):
        return jnp.where(lane < HD // 2, top, sums)

    def merge(buf, n):
        m = [buf[i, 1][:, :1] for i in range(n)]
        l = [buf[i, 1][:, HD - 1 :] for i in range(n)]
        top = functools.reduce(jnp.maximum, m)
        w = [jnp.exp(t - top) for t in m]
        sums = sum(a * b for a, b in zip(l, w))
        o = sum(buf[i, 0] * w[i] for i in range(n))
        return top, sums, o

    def tree(buf, n):
        parts = [buf[i] for i in range(n)]
        while len(parts) > 1:
            parts = [parts[i] + parts[i + 1] for i in range(0, len(parts), 2)]
        return parts[0]

    def decode_1():
        gathered(proj_row, row_peer, 2 * y + k, ROW - 1, peer_send, 0, pr_recv)
        proj_z[z] = tree(proj_row, ROW)
        spread(proj_z, z_peer, z, 3, peer_send, 7, pz_recv)

    def decode_2():
        gathered(proj_z, z_peer, z, 3, peer_send, 7, pz_recv)
        total = tree(proj_z, NZ)
        proj = total[:, : 6 * HD] * lax.rsqrt(total[:, 6 * HD :][:, :1] / width + EPS)
        sub = lax.broadcasted_iota(jnp.int32, (8, HD), 0)
        position = jnp.where(sub % 2 == 0, lens_ref[0], lens_ref[1]) + sub // 2
        angle = position.astype(F32) * freq_ref[...]
        cosine, sine = jnp.cos(angle), jnp.sin(angle)
        sine = jnp.where(lax.broadcasted_iota(jnp.int32, (8, HD), 1) < HD // 2, -sine, sine)

        def rotated(v):
            return (v * cosine + pltpu.roll(v, HD // 2, 1) * sine).astype(BF16)

        queries = jnp.concatenate([rotated(proj[:, h * HD : (h + 1) * HD]) for h in range(HEADS)], axis=0)
        blank = jnp.zeros((HD - 8, HD), F32)
        new_key = jnp.concatenate([rotated(proj[:, 4 * HD : 5 * HD]).astype(F32), blank], axis=0).astype(BF16)
        new_value = jnp.concatenate([proj[:, 5 * HD : 6 * HD], blank], axis=0).astype(BF16)
        own = kv_own[...].reshape(2 * ROWS, 2 * HD)
        keys = jnp.concatenate([own[:, :HD], new_key], axis=0)
        values = jnp.concatenate([own[:, HD:], new_value], axis=0)
        scores = lax.dot_general(queries, keys, NT, preferred_element_type=F32) * (1.0 / math.sqrt(HD))
        row = lax.broadcasted_iota(jnp.int32, scores.shape, 0) % 8
        col = lax.broadcasted_iota(jnp.int32, scores.shape, 1)
        new = col - 2 * ROWS
        limit = jnp.where(col < ROWS, lens_ref[0], lens_ref[1])
        old_ok = (col < 2 * ROWS) & (col // ROWS == row % 2) & (seq * ROWS + col % ROWS < limit)
        new_ok = (new >= 0) & (new <= row) & (new % 2 == row % 2) & (seq == 0)
        scores = jnp.where(old_ok | new_ok, scores, NEG)
        top = jnp.max(scores, axis=-1, keepdims=True)
        p = jnp.exp(scores - top)
        mine = 2 * y + k
        soft_row[mine, 0] = jnp.dot(p.astype(BF16), values, preferred_element_type=F32)
        soft_row[mine, 1] = packed(top, jnp.sum(p, axis=-1, keepdims=True))
        spread(soft_row, row_peer, mine, ROW - 1, peer_send, 10, sr_recv)

    def decode_3():
        gathered(soft_row, row_peer, 2 * y + k, ROW - 1, peer_send, 10, sr_recv)
        top, sums, o = merge(soft_row, ROW)
        soft_z[z, 0] = o
        soft_z[z, 1] = packed(top, sums)
        spread(soft_z, z_peer, z, 3, peer_send, 17, sz_recv)

    def decode_4():
        gathered(soft_z, z_peer, z, 3, peer_send, 17, sz_recv)
        _, sums, o = merge(soft_z, NZ)
        att = o / sums
        out = jnp.zeros((8, ROWS), F32)
        for h in range(HEADS):
            head = att[8 * h : 8 * h + 8].astype(BF16)
            out += jnp.dot(head, wout[h * HD : (h + 1) * HD, :], preferred_element_type=F32)
        out_tp[tp] = out
        spread(out_tp, tp_peer, tp, N_TP - 1, peer_send, 20, ot_recv)

    def decode_5():
        gathered(out_tp, tp_peer, tp, N_TP - 1, peer_send, 20, ot_recv)
        dec_ref[...] = (hid + tree(out_tp, N_TP)).astype(BF16)

    def far_first(zc):
        @pl.when(big == 1)
        def _():
            arrived(0, y, zc)
            hand_out(0, zc)

    def far_pass_on():
        @pl.when(big == 1)
        def _():
            pass_on(0, 0)
            pass_on(0, 1)

    def far_take(*which):
        @pl.when(big == 1)
        def _():
            for yp, zc in which:
                take(0, yp, zc)

    loads[3].wait()
    scale_queries(q_own, s)

    def by(i, values):
        out = values[-1]
        for j in range(len(values) - 2, -1, -1):
            out = jnp.where(i == j, values[j], out)
        return out

    def result(r, h):
        return (acc[r, h][:, :HD] / acc[r, h][:, HD:]).astype(BF16)

    back = copy(o_out, o_in, swap_send.at[2], swap_recv.at[1], pair)

    near_2 = 8 + EARLY
    far_2 = near_2 + 8
    far_3 = far_2 + NY

    @pl.loop(0, far_3 + NY - EARLY)
    def _(i):
        @pl.when(i == 1)
        def _():
            arrived(big, y, 1 - s)
            hand_out(big, 1 - s)

        @pl.when(i == 2)
        def _():
            pass_on(big, 0)
            pass_on(big, 1)

        @pl.when(i == 4)
        def _():
            take(big, y_minus, 1)
            take(big, y_plus, 0)
            far_first(s)
            decode_1()

        @pl.when(i == 6)
        def _():
            take(big, y_far, 0)
            take(big, y_far, 1)
            far_first(1 - s)

        @pl.when(i == 8)
        def _():
            decode_2()

            @pl.loop(1, N_SEQ)
            def _(d):
                page(lax.rem(seq + d, N_SEQ), seq).start()

        @pl.when(i == near_2)
        def _():
            far_pass_on()
            swap_q.wait_recv()
            scale_queries(q_in, 1 - s)

        @pl.when(i == near_2 + 2)
        def _():
            far_take((y_minus, 1), (y_plus, 0))

        @pl.when(i == near_2 + 4)
        def _():
            decode_3()

        @pl.when(i == near_2 + 6)
        def _():
            far_take((y_far, 0), (y_far, 1))

        @pl.when(i == far_2 + 1)
        def _():
            loads[4].wait()
            decode_4()

        @pl.when(i == far_3)
        def _():
            for h in range(HEADS):
                o_out[:, h * HD : (h + 1) * HD] = result(1 - s, h)
            back.start()

        j = jnp.where(i < 8, i, i - near_2)
        yp = lax.rem(y + by(j, [0, 0, 3, 1, 3, 1, 2, 2]), NY)
        zc = by(j, [s, 1 - s, 0, 1, 1, 0, 0, 1])
        r = jnp.where(i < 8, s, 1 - s)

        @pl.when(i < 8)
        def _():
            mate_arrived(big, yp, zc)

        @pl.when((i < 8) | ((i >= near_2) & (i < far_2)))
        def _():
            @pl.when(zc * NY + yp <= r * NY + y)
            def _():
                near_step(r, yp, zc)

        place = jnp.where(i < near_2, i - 8, jnp.where(i < far_3, i - far_2, i - far_3 + EARLY))
        far_yp = lax.rem(y + by(place, [0, 3, 1, 2]), NY)
        again = (i >= far_2) & (i < far_2 + EARLY) | (i >= far_3)
        early = (i >= 8) & (i < near_2)

        @pl.when((big == 1) & (early | (i >= far_2)))
        def _():
            @pl.when(jnp.logical_not(again))
            def _():
                mate_arrived(0, far_yp, 0)
                mate_arrived(0, far_yp, 1)

            far_step(jnp.where((i >= far_2) & (i < far_3), 1 - s, s), far_yp)

    for h in range(HEADS):
        o_own[:, h * HD : (h + 1) * HD] = result(s, h)
    stores = [
        pltpu.make_async_copy(src, dst, local.at[i])
        for i, (src, dst) in enumerate([(o_own, attn_ref.at[s]), (pages, pages_ref), (o_in, attn_ref.at[1 - s])])
    ]
    stores[0].start()
    decode_5()

    swap_kv.wait_send()
    swap_q.wait_send()
    own_page.wait()

    @pl.loop(1, N_SEQ)
    def _(d):
        page(lax.rem(seq + d, N_SEQ), lax.rem(seq + d, N_SEQ)).wait()

    stores[1].start()

    @pl.loop(0, 2)
    def _(zp):
        @pl.when(zp <= big)
        def _():
            for zc in (0, 1):
                for direction in (0, 1):
                    first(zp, direction, zc).wait_send()
                for yp in range(NY):
                    to_mate(zp, yp, zc).wait_send()
                forward(zp, zc).wait_send()

    @pl.when(big == 0)
    def _():
        far(0).wait_send()
        far(1).wait_send()

    back.wait()
    stores[2].start()
    for store in stores:
        store.wait()


def publish(attn_ref, pages_ref, dec_ref, attn_out, pages_out, dec_out, attn, pages, arrive, leave):
    pieces = [
        (attn_ref.at[p, pl.ds(r, HD)], attn.at[p, pl.ds(r, HD)], attn_out.at[p, pl.ds(r, HD)]) for p in (0, 1) for r in (0, HD)
    ]
    half = N_SEQ // 2
    pieces += [(pages_ref.at[pl.ds(r, half)], pages.at[pl.ds(r, half)], pages_out.at[pl.ds(r, half)]) for r in (0, half)]
    inward = [pltpu.make_async_copy(src, via, arrive.at[i]) for i, (src, via, _) in enumerate(pieces)]
    outward = [pltpu.make_async_copy(via, dst, leave.at[i]) for i, (_, via, dst) in enumerate(pieces)]
    for c in inward:
        c.start()
    for i in range(dec_out.shape[0]):
        dec_out[i] = dec_ref[2 * i : 2 * i + 2, :]
    for c, then in zip(inward, outward):
        c.wait()
        then.start()
    for c in outward:
        c.wait()


def on_device(q_prefill, kv_prefill, prompt_len, group_of, hidden, norm_gain, w_qkv, w_out):
    n_prompts, rows = q_prefill.shape[:2]
    cycle = lax.axis_size("seq")
    steps = hidden.shape[0]
    frequency = BASE ** (-2.0 * np.arange(HD // 2, dtype=np.float64) / HD)
    frequency = np.concatenate([frequency, frequency])[None].astype(np.float32)

    vmem = pl.BlockSpec(memory_space=pltpu.VMEM)
    smem = pl.BlockSpec(memory_space=pltpu.SMEM)
    hbm = pl.BlockSpec(memory_space=pltpu.HBM)
    dma = pltpu.SemaphoreType.DMA
    width = hidden.shape[2] * cycle
    attn, pages, decoded = pl.pallas_call(
        functools.partial(kernel, float(width)),
        out_shape=(
            jax.ShapeDtypeStruct((n_prompts, rows, HEADS * HD), BF16),
            jax.ShapeDtypeStruct((N_SEQ, PIECE, 2 * HD), BF16),
            jax.ShapeDtypeStruct((steps * n_prompts, rows), BF16),
        ),
        in_specs=[smem, smem, hbm, hbm, vmem, vmem, hbm, hbm, vmem],
        out_specs=(hbm, hbm, vmem),
        scratch_shapes=[
            pltpu.VMEM((2, NY, 2, 2, ROWS, 2 * HD), BF16),
            pltpu.VMEM((2, ROWS, 2 * HD), BF16),
            pltpu.VMEM((ROWS, HEADS * HD), BF16),
            pltpu.VMEM((ROWS, HEADS * HD), BF16),
            pltpu.VMEM((ROWS, 6 * HD), BF16),
            pltpu.VMEM((HEADS * HD, ROWS), BF16),
            pltpu.VMEM((2, HEADS, ROWS, 2 * HD), BF16),
            pltpu.VMEM((2, HEADS, ROWS, 2 * HD), F32),
            pltpu.VMEM((2, HEADS, ROWS, HD), F32),
            pltpu.VMEM((ROWS, HEADS * HD), BF16),
            pltpu.VMEM((ROWS, HEADS * HD), BF16),
            pltpu.VMEM((ROWS, HEADS * HD), BF16),
            pltpu.VMEM((ROW, 8, 7 * HD), F32),
            pltpu.VMEM((NZ, 8, 7 * HD), F32),
            pltpu.VMEM((ROW, 2, 32, HD), F32),
            pltpu.VMEM((NZ, 2, 32, HD), F32),
            pltpu.VMEM((N_TP, 8, ROWS), F32),
            pltpu.VMEM((2, N_SEQ // 2, PIECE, 2 * HD), BF16),
            pltpu.VMEM((N_SEQ, PIECE, 2 * HD), BF16),
            dma((6,)), dma((3,)), dma((2,)), dma((2, NY, 2)), dma((2, NY, 2)),
            dma((2, 2, 2)), dma((2, 2)), dma((2, NY, 2)), dma((2,)),
            dma((27,)), dma((ROW,)), dma((NZ,)), dma((ROW,)), dma((NZ,)), dma((N_TP,)),
            dma((N_SEQ,)), dma((N_SEQ,)),
        ],
        compiler_params=pltpu.CompilerParams(
            collective_id=0, has_side_effects=True, vmem_limit_bytes=62 * 1024 * 1024
        ),
        cost_estimate=pl.CostEstimate(flops=9 * 10**9, bytes_accessed=3 * 10**6, transcendentals=17 * 10**6),
    )(
        prompt_len,
        group_of,
        q_prefill.reshape(n_prompts, rows, HEADS * HD),
        kv_prefill.reshape(n_prompts, rows, 2 * HD),
        hidden,
        norm_gain.reshape(1, rows),
        w_qkv.reshape(rows, 6 * HD),
        w_out.reshape(HEADS * HD, rows),
        frequency,
    )
    attn, pages, decoded = pl.pallas_call(
        publish,
        out_shape=(
            jax.ShapeDtypeStruct(attn.shape, BF16),
            jax.ShapeDtypeStruct(pages.shape, BF16),
            jax.ShapeDtypeStruct(hidden.shape, BF16),
        ),
        in_specs=[hbm, hbm, vmem],
        out_specs=(hbm, hbm, vmem),
        scratch_shapes=[pltpu.VMEM(attn.shape, BF16), pltpu.VMEM(pages.shape, BF16), dma((6,)), dma((6,))],
        compiler_params=pltpu.CompilerParams(vmem_limit_bytes=62 * 1024 * 1024),
    )(attn, pages, decoded)
    return (
        attn.reshape(n_prompts, rows, 1, HEADS * HD),
        pages.reshape(N_SEQ * PIECE, 1, 2 * HD),
        decoded,
    )


def solution(mesh):
    placed = (
        P(None, "seq", "tp", None),
        P(None, "seq", "tp", None),
        P(),
        P(),
        P(None, None, "seq"),
        P("seq"),
        P("seq", "tp", None),
        P("tp", None, "seq"),
    )
    return jax.shard_map(
        on_device,
        mesh=mesh,
        in_specs=placed,
        out_specs=(P(None, "seq", "tp", None), P("seq", "tp", None), P(None, None, "seq")),
        check_vma=False,
    )
```

```python
import functools
import math

import jax
import jax.numpy as jnp
import numpy as np
from jax import lax
from jax.experimental import pallas as pl
from jax.experimental.pallas import tpu as pltpu
from jax.sharding import PartitionSpec as P

MESH = pl.DeviceIdType.MESH
NEG = -1e30
EPS = 1e-05
BASE = 500000.0
ROWS = 256
BLOCK = 512
HD = 128
HEADS = 4
NY = 4
NZ = 4
ROW = 8
N_TP = 8
EARLY = 0
N_SEQ = 32
PIECE = 16
BF16 = jnp.bfloat16
F32 = jnp.float32
NT = (((1,), (1,)), ((), ()))


def kernel(
    width,
    lens_ref, group_ref, q_ref, kv_ref, hid_ref, gain_ref, wqkv_ref, wout_ref, freq_ref,
    attn_ref, pages_ref, dec_ref,
    blocks, kv_own, q_own, q_in, wqkv, wout, q_scaled, acc, tops, o_in, o_out,
    proj_row, proj_z, soft_row, soft_z, out_tp, by_group, pages,
    local, swap_send, swap_recv, chunk_recv, chip_recv,
    first_send, forward_send, chip_send, far_send,
    peer_send, pr_recv, pz_recv, sr_recv, sz_recv, ot_recv,
    page_send, page_recv,
):
    seq = lax.axis_index("seq")
    tp = lax.axis_index("tp")
    z, y, k = seq // 8, (seq // 2) % NY, seq % 2
    big, s = z // 2, z % 2
    other = 1 - k

    def on(zz, yy, core):
        return {"seq": zz * 8 + yy * 2 + core, "tp": tp}

    mate = on(z, y, other)
    pair = on(big * 2 + 1 - s, y, k)
    up, down = on(z, lax.rem(y + 1, NY), k), on(z, lax.rem(y + 3, NY), k)

    def row_peer(d):
        place = lax.rem(2 * y + k + d, ROW)
        return on(z, place // 2, lax.rem(place, 2))

    def z_peer(d):
        return on(lax.rem(z + d, NZ), y, k)

    def tp_peer(d):
        return {"seq": seq, "tp": lax.rem(tp + d, N_TP)}

    def copy(src, dst, ssem, rsem, dev):
        return pltpu.make_async_remote_copy(
            src_ref=src, dst_ref=dst, send_sem=ssem, recv_sem=rsem, device_id=dev, device_id_type=MESH
        )

    loads = [
        pltpu.make_async_copy(src, dst, local.at[i])
        for i, (src, dst) in enumerate([
            (kv_ref, kv_own), (kv_ref.at[s], blocks.at[big, y, s, k]), (wqkv_ref, wqkv),
            (q_ref.at[s], q_own), (wout_ref, wout),
        ])
    ]
    for load in loads:
        load.start()

    barrier = pltpu.get_barrier_semaphore()

    @pl.loop(1, N_TP)
    def _(d):
        pl.semaphore_signal(barrier, inc=1, device_id=tp_peer(d), device_id_type=MESH)

    @pl.loop(1, N_SEQ)
    def _(d):
        dev = {"seq": lax.rem(seq + d, N_SEQ), "tp": tp}
        pl.semaphore_signal(barrier, inc=1, device_id=dev, device_id_type=MESH)

    acc[...] = jnp.zeros_like(acc)
    tops[...] = jnp.full_like(tops, NEG)

    loads[0].wait()
    second = (group_ref[0] != 0).astype(jnp.int32)
    by_group[0] = kv_own[second].reshape(N_SEQ // 2, PIECE, 2 * HD)
    by_group[1] = kv_own[1 - second].reshape(N_SEQ // 2, PIECE, 2 * HD)

    def page(owner, source):
        return copy(
            by_group.at[owner // 16, lax.rem(owner, 16)], pages.at[source],
            page_send.at[owner], page_recv.at[source], {"seq": owner, "tp": tp},
        )

    loads[2].wait()
    hid = jnp.concatenate([hid_ref[i].astype(F32) for i in range(hid_ref.shape[0])], axis=0)
    squares = jnp.sum(hid * hid, axis=-1, keepdims=True)
    scaled_in = (hid * gain_ref[...]).astype(BF16)
    part = jnp.dot(scaled_in, wqkv[...], preferred_element_type=F32)
    proj_row[2 * y + k] = jnp.concatenate([part, jnp.broadcast_to(squares, (8, HD))], axis=1)
    loads[1].wait()

    def chunk(zp, yp, zc, ssem, dev, to_mate=False):
        ref = blocks.at[zp, yp, zc, k]
        return copy(ref, ref, ssem, (chip_recv if to_mate else chunk_recv).at[zp, yp, zc], dev)

    def to_mate(zp, yp, zc):
        return chunk(zp, yp, zc, chip_send.at[zp, yp, zc], mate, True)

    def first(zp, direction, zc):
        return chunk(zp, y, zc, first_send.at[zp, direction, zc], (up, down)[direction])

    y_minus, y_plus, y_far = lax.rem(y + 3, NY), lax.rem(y + 1, NY), lax.rem(y + 2, NY)

    def forward(zp, direction):
        return chunk(zp, (y_minus, y_plus)[direction], direction, forward_send.at[zp, direction], (up, down)[direction])

    def far(prompt):
        return copy(
            kv_ref.at[prompt], blocks.at[0, y, s, k], far_send.at[prompt], chunk_recv.at[0, y, s], on(2 + prompt, y, k)
        )

    def arrived(zp, yp, zc):
        chunk(zp, yp, zc, chip_send.at[0, 0, 0], mate).wait_recv()

    def mate_arrived(zp, yp, zc):
        ref = blocks.at[zp, yp, zc, other]
        copy(ref, ref, chip_send.at[0, 0, 0], chip_recv.at[zp, yp, zc], mate).wait_recv()

    def hand_out(zp, zc):
        first(zp, 0, zc).start()
        first(zp, 1, zc).start()
        to_mate(zp, y, zc).start()

    def pass_on(zp, direction):
        yp = (y_minus, y_plus)[direction]
        arrived(zp, yp, direction)
        forward(zp, direction).start()
        to_mate(zp, yp, direction).start()

    def take(zp, yp, zc):
        arrived(zp, yp, zc)
        to_mate(zp, yp, zc).start()

    swap_kv = copy(
        kv_ref.at[1 - s], blocks.at[big, y, s, k], swap_send.at[0], chunk_recv.at[big, y, s], pair
    )
    swap_q = copy(q_ref.at[1 - s], q_in, swap_send.at[1], swap_recv.at[0], pair)

    pl.semaphore_wait(barrier, N_TP + N_SEQ - 2)

    swap_kv.start()
    hand_out(big, s)

    @pl.when(big == 0)
    def _():
        far(0).start()
        far(1).start()

    swap_q.start()
    own_page = pltpu.make_async_copy(by_group.at[seq // 16, lax.rem(seq, 16)], pages.at[seq], local.at[5])
    own_page.start()

    def spread(buf, peer, mine, n_peers, sends, first, recv):
        for d in range(1, n_peers + 1):
            copy(buf.at[mine], buf.at[mine], sends.at[first + d - 1], recv.at[mine], peer(d)).start()

    def gathered(buf, peer, mine, n_peers, sends, first, recv):
        for d in range(1, n_peers + 1):
            src = lax.rem(mine + d, n_peers + 1)
            c = copy(buf.at[src], buf.at[src], sends.at[first + d - 1], recv.at[src], peer(d))
            c.wait()

    spread(proj_row, row_peer, 2 * y + k, ROW - 1, peer_send, 0, pr_recv)

    def scale_queries(ref, r):
        c = math.log2(math.e) / math.sqrt(HD)
        for h in range(HEADS):
            wide = ref[:, h * HD : (h + 1) * HD].astype(F32) * c
            top = wide.astype(BF16)
            q_scaled[r, h] = jnp.concatenate([top, (wide - top.astype(F32)).astype(BF16)], axis=1)

    length = lens_ref[s]

    def attend(r, rows, bias):
        n = rows.shape[0]
        keys, values = rows[:, :HD], rows[:, HD:]
        keys = jnp.concatenate([keys, keys], axis=1)
        values = jnp.concatenate([values, jnp.ones((n, HD), BF16)], axis=1)

        def scores(h):
            return lax.dot_general(q_scaled[r, h], keys, NT, preferred_element_type=F32) + bias

        now_scores = scores(0)
        for h in range(HEADS):
            ahead = scores(h + 1) if h + 1 < HEADS else None
            before = tops[r, h]
            now = jnp.maximum(before, jnp.max(now_scores, axis=-1, keepdims=True))
            p = jnp.exp2(now_scores - jnp.concatenate([now] * (n // HD), axis=1)).astype(BF16)
            shrink = jnp.exp2(before - now)
            tops[r, h] = now
            o = jnp.dot(p, values, preferred_element_type=F32)
            acc[r, h] = acc[r, h] * jnp.concatenate([shrink, shrink], axis=1) + o
            now_scores = ahead

    def near_step(r, yp, zc):
        key_at = ((2 * big + zc) * NY + yp) * BLOCK
        row_at = ((2 * big + r) * NY + y) * BLOCK + k * ROWS
        row = row_at + lax.broadcasted_iota(jnp.int32, (ROWS, BLOCK), 0)
        col = key_at + lax.broadcasted_iota(jnp.int32, (ROWS, BLOCK), 1)
        bias = jnp.where(col < jnp.minimum(row + 1, length), 0.0, NEG)
        attend(r, blocks[big, yp, zc].reshape(BLOCK, 2 * HD), bias)

    def far_step(r, yp):
        attend(r, blocks[0, yp].reshape(2 * BLOCK, 2 * HD), 0.0)

    lane = lax.broadcasted_iota(jnp.int32, (32, HD), 1)

    def packed(top, sums):
        return jnp.where(lane < HD // 2, top, sums)

    def merge(buf, n):
        m = [buf[i, 1][:, :1] for i in range(n)]
        l = [buf[i, 1][:, HD - 1 :] for i in range(n)]
        top = functools.reduce(jnp.maximum, m)
        w = [jnp.exp(t - top) for t in m]
        sums = sum(a * b for a, b in zip(l, w))
        o = sum(buf[i, 0] * w[i] for i in range(n))
        return top, sums, o

    def tree(buf, n):
        parts = [buf[i] for i in range(n)]
        while len(parts) > 1:
            parts = [parts[i] + parts[i + 1] for i in range(0, len(parts), 2)]
        return parts[0]

    def decode_1():
        gathered(proj_row, row_peer, 2 * y + k, ROW - 1, peer_send, 0, pr_recv)
        proj_z[z] = tree(proj_row, ROW)
        spread(proj_z, z_peer, z, 3, peer_send, 7, pz_recv)

    def decode_2():
        gathered(proj_z, z_peer, z, 3, peer_send, 7, pz_recv)
        total = tree(proj_z, NZ)
        proj = total[:, : 6 * HD] * lax.rsqrt(total[:, 6 * HD :][:, :1] / width + EPS)
        sub = lax.broadcasted_iota(jnp.int32, (8, HD), 0)
        position = jnp.where(sub % 2 == 0, lens_ref[0], lens_ref[1]) + sub // 2
        angle = position.astype(F32) * freq_ref[...]
        cosine, sine = jnp.cos(angle), jnp.sin(angle)
        sine = jnp.where(lax.broadcasted_iota(jnp.int32, (8, HD), 1) < HD // 2, -sine, sine)

        def rotated(v):
            return (v * cosine + pltpu.roll(v, HD // 2, 1) * sine).astype(BF16)

        queries = jnp.concatenate([rotated(proj[:, h * HD : (h + 1) * HD]) for h in range(HEADS)], axis=0)
        blank = jnp.zeros((HD - 8, HD), F32)
        new_key = jnp.concatenate([rotated(proj[:, 4 * HD : 5 * HD]).astype(F32), blank], axis=0).astype(BF16)
        new_value = jnp.concatenate([proj[:, 5 * HD : 6 * HD], blank], axis=0).astype(BF16)
        own = kv_own[...].reshape(2 * ROWS, 2 * HD)
        keys = jnp.concatenate([own[:, :HD], new_key], axis=0)
        values = jnp.concatenate([own[:, HD:], new_value], axis=0)
        scores = lax.dot_general(queries, keys, NT, preferred_element_type=F32) * (1.0 / math.sqrt(HD))
        row = lax.broadcasted_iota(jnp.int32, scores.shape, 0) % 8
        col = lax.broadcasted_iota(jnp.int32, scores.shape, 1)
        new = col - 2 * ROWS
        limit = jnp.where(col < ROWS, lens_ref[0], lens_ref[1])
        old_ok = (col < 2 * ROWS) & (col // ROWS == row % 2) & (seq * ROWS + col % ROWS < limit)
        new_ok = (new >= 0) & (new <= row) & (new % 2 == row % 2) & (seq == 0)
        scores = jnp.where(old_ok | new_ok, scores, NEG)
        top = jnp.max(scores, axis=-1, keepdims=True)
        p = jnp.exp(scores - top)
        mine = 2 * y + k
        soft_row[mine, 0] = jnp.dot(p.astype(BF16), values, preferred_element_type=F32)
        soft_row[mine, 1] = packed(top, jnp.sum(p, axis=-1, keepdims=True))
        spread(soft_row, row_peer, mine, ROW - 1, peer_send, 10, sr_recv)

    def decode_3():
        gathered(soft_row, row_peer, 2 * y + k, ROW - 1, peer_send, 10, sr_recv)
        top, sums, o = merge(soft_row, ROW)
        soft_z[z, 0] = o
        soft_z[z, 1] = packed(top, sums)
        spread(soft_z, z_peer, z, 3, peer_send, 17, sz_recv)

    def decode_4():
        gathered(soft_z, z_peer, z, 3, peer_send, 17, sz_recv)
        _, sums, o = merge(soft_z, NZ)
        att = o / sums
        out = jnp.zeros((8, ROWS), F32)
        for h in range(HEADS):
            head = att[8 * h : 8 * h + 8].astype(BF16)
            out += jnp.dot(head, wout[h * HD : (h + 1) * HD, :], preferred_element_type=F32)
        out_tp[tp] = out
        spread(out_tp, tp_peer, tp, N_TP - 1, peer_send, 20, ot_recv)

    def decode_5():
        gathered(out_tp, tp_peer, tp, N_TP - 1, peer_send, 20, ot_recv)
        dec_ref[...] = (hid + tree(out_tp, N_TP)).astype(BF16)

    def far_first(zc):
        @pl.when(big == 1)
        def _():
            arrived(0, y, zc)
            hand_out(0, zc)

    def far_pass_on():
        @pl.when(big == 1)
        def _():
            pass_on(0, 0)
            pass_on(0, 1)

    def far_take(*which):
        @pl.when(big == 1)
        def _():
            for yp, zc in which:
                take(0, yp, zc)

    loads[3].wait()
    scale_queries(q_own, s)

    def by(i, values):
        out = values[-1]
        for j in range(len(values) - 2, -1, -1):
            out = jnp.where(i == j, values[j], out)
        return out

    def result(r, h):
        return (acc[r, h][:, :HD] / acc[r, h][:, HD:]).astype(BF16)

    back = copy(o_out, o_in, swap_send.at[2], swap_recv.at[1], pair)

    near_2 = 8 + EARLY
    far_2 = near_2 + 8
    far_3 = far_2 + NY

    @pl.loop(0, far_3 + NY - EARLY)
    def _(i):
        @pl.when(i == 1)
        def _():
            arrived(big, y, 1 - s)
            hand_out(big, 1 - s)

        @pl.when(i == 2)
        def _():
            pass_on(big, 0)
            pass_on(big, 1)

        @pl.when(i == 4)
        def _():
            take(big, y_minus, 1)
            take(big, y_plus, 0)
            far_first(s)
            decode_1()

        @pl.when(i == 6)
        def _():
            take(big, y_far, 0)
            take(big, y_far, 1)
            far_first(1 - s)

        @pl.when(i == 8)
        def _():
            decode_2()

            @pl.loop(1, N_SEQ)
            def _(d):
                page(lax.rem(seq + d, N_SEQ), seq).start()

        @pl.when(i == near_2)
        def _():
            far_pass_on()
            swap_q.wait_recv()
            scale_queries(q_in, 1 - s)

        @pl.when(i == near_2 + 2)
        def _():
            far_take((y_minus, 1), (y_plus, 0))

        @pl.when(i == near_2 + 4)
        def _():
            decode_3()

        @pl.when(i == near_2 + 6)
        def _():
            far_take((y_far, 0), (y_far, 1))

        @pl.when(i == far_2 + 1)
        def _():
            loads[4].wait()
            decode_4()

        @pl.when(i == far_3)
        def _():
            for h in range(HEADS):
                o_out[:, h * HD : (h + 1) * HD] = result(1 - s, h)
            back.start()

        j = jnp.where(i < 8, i, i - near_2)
        yp = lax.rem(y + by(j, [0, 0, 3, 1, 3, 1, 2, 2]), NY)
        zc = by(j, [s, 1 - s, 0, 1, 1, 0, 0, 1])
        r = jnp.where(i < 8, s, 1 - s)

        @pl.when(i < 8)
        def _():
            mate_arrived(big, yp, zc)

        @pl.when((i < 8) | ((i >= near_2) & (i < far_2)))
        def _():
            @pl.when(zc * NY + yp <= r * NY + y)
            def _():
                near_step(r, yp, zc)

        place = jnp.where(i < near_2, i - 8, jnp.where(i < far_3, i - far_2, i - far_3 + EARLY))
        far_yp = lax.rem(y + by(place, [0, 3, 1, 2]), NY)
        again = (i >= far_2) & (i < far_2 + EARLY) | (i >= far_3)
        early = (i >= 8) & (i < near_2)

        @pl.when((big == 1) & (early | (i >= far_2)))
        def _():
            @pl.when(jnp.logical_not(again))
            def _():
                mate_arrived(0, far_yp, 0)
                mate_arrived(0, far_yp, 1)

            far_step(jnp.where((i >= far_2) & (i < far_3), 1 - s, s), far_yp)

    for h in range(HEADS):
        attn_ref[s, :, h * HD : (h + 1) * HD] = result(s, h)
    decode_5()

    swap_kv.wait_send()
    swap_q.wait_send()
    own_page.wait()

    @pl.loop(1, N_SEQ)
    def _(d):
        page(lax.rem(seq + d, N_SEQ), lax.rem(seq + d, N_SEQ)).wait()

    pages_ref[...] = pages[...]

    @pl.loop(0, 2)
    def _(zp):
        @pl.when(zp <= big)
        def _():
            for zc in (0, 1):
                for direction in (0, 1):
                    first(zp, direction, zc).wait_send()
                for yp in range(NY):
                    to_mate(zp, yp, zc).wait_send()
                forward(zp, zc).wait_send()

    @pl.when(big == 0)
    def _():
        far(0).wait_send()
        far(1).wait_send()

    back.wait()
    attn_ref[1 - s] = o_in[...]


def publish(attn_ref, pages_ref, dec_ref, attn_out, pages_out, dec_out, leave):
    pieces = [(attn_ref.at[0], attn_out.at[0]), (attn_ref.at[1], attn_out.at[1]), (pages_ref, pages_out)]
    outward = [pltpu.make_async_copy(src, dst, leave.at[i]) for i, (src, dst) in enumerate(pieces)]
    for c in outward:
        c.start()
    for i in range(dec_out.shape[0]):
        dec_out[i] = dec_ref[2 * i : 2 * i + 2, :]
    for c in outward:
        c.wait()


def on_device(q_prefill, kv_prefill, prompt_len, group_of, hidden, norm_gain, w_qkv, w_out):
    n_prompts, rows = q_prefill.shape[:2]
    cycle = lax.axis_size("seq")
    steps = hidden.shape[0]
    frequency = BASE ** (-2.0 * np.arange(HD // 2, dtype=np.float64) / HD)
    frequency = np.concatenate([frequency, frequency])[None].astype(np.float32)

    vmem = pl.BlockSpec(memory_space=pltpu.VMEM)
    smem = pl.BlockSpec(memory_space=pltpu.SMEM)
    hbm = pl.BlockSpec(memory_space=pltpu.HBM)
    dma = pltpu.SemaphoreType.DMA
    width = hidden.shape[2] * cycle
    attn, pages, decoded = pl.pallas_call(
        functools.partial(kernel, float(width)),
        out_shape=(
            pltpu.VMEM((n_prompts, rows, HEADS * HD), BF16),
            pltpu.VMEM((N_SEQ, PIECE, 2 * HD), BF16),
            pltpu.VMEM((steps * n_prompts, rows), BF16),
        ),
        in_specs=[smem, smem, hbm, hbm, vmem, vmem, hbm, hbm, vmem],
        out_specs=(vmem, vmem, vmem),
        scratch_shapes=[
            pltpu.VMEM((2, NY, 2, 2, ROWS, 2 * HD), BF16),
            pltpu.VMEM((2, ROWS, 2 * HD), BF16),
            pltpu.VMEM((ROWS, HEADS * HD), BF16),
            pltpu.VMEM((ROWS, HEADS * HD), BF16),
            pltpu.VMEM((ROWS, 6 * HD), BF16),
            pltpu.VMEM((HEADS * HD, ROWS), BF16),
            pltpu.VMEM((2, HEADS, ROWS, 2 * HD), BF16),
            pltpu.VMEM((2, HEADS, ROWS, 2 * HD), F32),
            pltpu.VMEM((2, HEADS, ROWS, HD), F32),
            pltpu.VMEM((ROWS, HEADS * HD), BF16),
            pltpu.VMEM((ROWS, HEADS * HD), BF16),
            pltpu.VMEM((ROW, 8, 7 * HD), F32),
            pltpu.VMEM((NZ, 8, 7 * HD), F32),
            pltpu.VMEM((ROW, 2, 32, HD), F32),
            pltpu.VMEM((NZ, 2, 32, HD), F32),
            pltpu.VMEM((N_TP, 8, ROWS), F32),
            pltpu.VMEM((2, N_SEQ // 2, PIECE, 2 * HD), BF16),
            pltpu.VMEM((N_SEQ, PIECE, 2 * HD), BF16),
            dma((6,)), dma((3,)), dma((2,)), dma((2, NY, 2)), dma((2, NY, 2)),
            dma((2, 2, 2)), dma((2, 2)), dma((2, NY, 2)), dma((2,)),
            dma((27,)), dma((ROW,)), dma((NZ,)), dma((ROW,)), dma((NZ,)), dma((N_TP,)),
            dma((N_SEQ,)), dma((N_SEQ,)),
        ],
        compiler_params=pltpu.CompilerParams(
            collective_id=0, has_side_effects=True, vmem_limit_bytes=60 * 1024 * 1024
        ),
        cost_estimate=pl.CostEstimate(flops=9 * 10**9, bytes_accessed=3 * 10**6, transcendentals=17 * 10**6),
    )(
        prompt_len,
        group_of,
        q_prefill.reshape(n_prompts, rows, HEADS * HD),
        kv_prefill.reshape(n_prompts, rows, 2 * HD),
        hidden,
        norm_gain.reshape(1, rows),
        w_qkv.reshape(rows, 6 * HD),
        w_out.reshape(HEADS * HD, rows),
        frequency,
    )
    attn, pages, decoded = pl.pallas_call(
        publish,
        out_shape=(
            jax.ShapeDtypeStruct(attn.shape, BF16),
            jax.ShapeDtypeStruct(pages.shape, BF16),
            jax.ShapeDtypeStruct(hidden.shape, BF16),
        ),
        in_specs=[vmem, vmem, vmem],
        out_specs=(hbm, hbm, vmem),
        scratch_shapes=[dma((3,))],
        compiler_params=pltpu.CompilerParams(vmem_limit_bytes=16 * 1024 * 1024),
    )(attn, pages, decoded)
    return (
        attn.reshape(n_prompts, rows, 1, HEADS * HD),
        pages.reshape(N_SEQ * PIECE, 1, 2 * HD),
        decoded,
    )


def solution(mesh):
    placed = (
        P(None, "seq", "tp", None),
        P(None, "seq", "tp", None),
        P(),
        P(),
        P(None, None, "seq"),
        P("seq"),
        P("seq", "tp", None),
        P("tp", None, "seq"),
    )
    return jax.shard_map(
        on_device,
        mesh=mesh,
        in_specs=placed,
        out_specs=(P(None, "seq", "tp", None), P("seq", "tp", None), P(None, None, "seq")),
        check_vma=False,
    )
```

```python
import functools
import math

import jax
import jax.numpy as jnp
import numpy as np
from jax import lax
from jax.experimental import pallas as pl
from jax.experimental.pallas import tpu as pltpu
from jax.sharding import PartitionSpec as P

MESH = pl.DeviceIdType.MESH
NEG = -1e30
EPS = 1e-05
BASE = 500000.0
ROWS = 256
BLOCK = 512
HD = 128
HEADS = 4
NY = 4
NZ = 4
ROW = 8
N_TP = 8
EARLY = 0
N_SEQ = 32
PIECE = 16
BF16 = jnp.bfloat16
F32 = jnp.float32
NT = (((1,), (1,)), ((), ()))


def kernel(
    width,
    lens_ref, group_ref, q_ref, kv_ref, hid_ref, gain_ref, wqkv_ref, wout_ref, freq_ref,
    attn_ref, pages_ref, dec_ref,
    blocks, kv_own, q_own, q_in, wqkv, wout, q_scaled, acc, tops, o_in, o_out,
    proj_row, proj_z, soft_row, soft_z, out_tp, by_group, pages,
    local, swap_send, swap_recv, chunk_recv, chip_recv,
    first_send, forward_send, chip_send, far_send,
    peer_send, pr_recv, pz_recv, sr_recv, sz_recv, ot_recv,
    page_send, page_recv,
):
    seq = lax.axis_index("seq")
    tp = lax.axis_index("tp")
    z, y, k = seq // 8, (seq // 2) % NY, seq % 2
    big, s = z // 2, z % 2
    other = 1 - k

    def on(zz, yy, core):
        return {"seq": zz * 8 + yy * 2 + core, "tp": tp}

    mate = on(z, y, other)
    pair = on(big * 2 + 1 - s, y, k)
    up, down = on(z, lax.rem(y + 1, NY), k), on(z, lax.rem(y + 3, NY), k)

    def row_peer(d):
        place = lax.rem(2 * y + k + d, ROW)
        return on(z, place // 2, lax.rem(place, 2))

    def z_peer(d):
        return on(lax.rem(z + d, NZ), y, k)

    def tp_peer(d):
        return {"seq": seq, "tp": lax.rem(tp + d, N_TP)}

    def copy(src, dst, ssem, rsem, dev):
        return pltpu.make_async_remote_copy(
            src_ref=src, dst_ref=dst, send_sem=ssem, recv_sem=rsem, device_id=dev, device_id_type=MESH
        )

    loads = [
        pltpu.make_async_copy(src, dst, local.at[i])
        for i, (src, dst) in enumerate([
            (kv_ref, kv_own), (kv_ref.at[s], blocks.at[big, y, s, k]), (wqkv_ref, wqkv),
            (q_ref.at[s], q_own), (wout_ref, wout),
        ])
    ]
    for load in loads:
        load.start()

    barrier = pltpu.get_barrier_semaphore()

    @pl.loop(1, N_TP)
    def _(d):
        pl.semaphore_signal(barrier, inc=1, device_id=tp_peer(d), device_id_type=MESH)

    @pl.loop(1, N_SEQ)
    def _(d):
        dev = {"seq": lax.rem(seq + d, N_SEQ), "tp": tp}
        pl.semaphore_signal(barrier, inc=1, device_id=dev, device_id_type=MESH)

    acc[...] = jnp.zeros_like(acc)
    tops[...] = jnp.full_like(tops, NEG)

    loads[0].wait()
    second = (group_ref[0] != 0).astype(jnp.int32)
    by_group[0] = kv_own[second].reshape(N_SEQ // 2, PIECE, 2 * HD)
    by_group[1] = kv_own[1 - second].reshape(N_SEQ // 2, PIECE, 2 * HD)

    def page(owner, source):
        return copy(
            by_group.at[owner // 16, lax.rem(owner, 16)], pages.at[source],
            page_send.at[owner], page_recv.at[source], {"seq": owner, "tp": tp},
        )

    loads[2].wait()
    hid = jnp.concatenate([hid_ref[i].astype(F32) for i in range(hid_ref.shape[0])], axis=0)
    squares = jnp.sum(hid * hid, axis=-1, keepdims=True)
    scaled_in = (hid * gain_ref[...]).astype(BF16)
    part = jnp.dot(scaled_in, wqkv[...], preferred_element_type=F32)
    proj_row[2 * y + k] = jnp.concatenate([part, jnp.broadcast_to(squares, (8, HD))], axis=1)
    loads[1].wait()

    def chunk(zp, yp, zc, ssem, dev, to_mate=False):
        ref = blocks.at[zp, yp, zc, k]
        return copy(ref, ref, ssem, (chip_recv if to_mate else chunk_recv).at[zp, yp, zc], dev)

    def to_mate(zp, yp, zc):
        return chunk(zp, yp, zc, chip_send.at[zp, yp, zc], mate, True)

    def first(zp, direction, zc):
        return chunk(zp, y, zc, first_send.at[zp, direction, zc], (up, down)[direction])

    y_minus, y_plus, y_far = lax.rem(y + 3, NY), lax.rem(y + 1, NY), lax.rem(y + 2, NY)

    def forward(zp, direction):
        return chunk(zp, (y_minus, y_plus)[direction], direction, forward_send.at[zp, direction], (up, down)[direction])

    def far(prompt):
        return copy(
            kv_ref.at[prompt], blocks.at[0, y, s, k], far_send.at[prompt], chunk_recv.at[0, y, s], on(2 + prompt, y, k)
        )

    def arrived(zp, yp, zc):
        chunk(zp, yp, zc, chip_send.at[0, 0, 0], mate).wait_recv()

    def mate_arrived(zp, yp, zc):
        ref = blocks.at[zp, yp, zc, other]
        copy(ref, ref, chip_send.at[0, 0, 0], chip_recv.at[zp, yp, zc], mate).wait_recv()

    def hand_out(zp, zc):
        first(zp, 0, zc).start()
        first(zp, 1, zc).start()
        to_mate(zp, y, zc).start()

    def pass_on(zp, direction):
        yp = (y_minus, y_plus)[direction]
        arrived(zp, yp, direction)
        forward(zp, direction).start()
        to_mate(zp, yp, direction).start()

    def take(zp, yp, zc):
        arrived(zp, yp, zc)
        to_mate(zp, yp, zc).start()

    swap_kv = copy(
        kv_ref.at[1 - s], blocks.at[big, y, s, k], swap_send.at[0], chunk_recv.at[big, y, s], pair
    )
    swap_q = copy(q_ref.at[1 - s], q_in, swap_send.at[1], swap_recv.at[0], pair)

    def scale_queries(ref, r):
        c = math.log2(math.e) / math.sqrt(HD)
        for h in range(HEADS):
            wide = ref[:, h * HD : (h + 1) * HD].astype(F32) * c
            top = wide.astype(BF16)
            q_scaled[r, h] = jnp.concatenate([top, (wide - top.astype(F32)).astype(BF16)], axis=1)

    loads[3].wait()
    scale_queries(q_own, s)
    pl.semaphore_wait(barrier, N_TP + N_SEQ - 2)

    swap_kv.start()
    hand_out(big, s)

    @pl.when(big == 0)
    def _():
        far(0).start()
        far(1).start()

    swap_q.start()
    own_page = pltpu.make_async_copy(by_group.at[seq // 16, lax.rem(seq, 16)], pages.at[seq], local.at[5])
    own_page.start()

    def spread(buf, peer, mine, n_peers, sends, first, recv):
        for d in range(1, n_peers + 1):
            copy(buf.at[mine], buf.at[mine], sends.at[first + d - 1], recv.at[mine], peer(d)).start()

    def gathered(buf, peer, mine, n_peers, sends, first, recv):
        for d in range(1, n_peers + 1):
            src = lax.rem(mine + d, n_peers + 1)
            c = copy(buf.at[src], buf.at[src], sends.at[first + d - 1], recv.at[src], peer(d))
            c.wait()

    spread(proj_row, row_peer, 2 * y + k, ROW - 1, peer_send, 0, pr_recv)

    length = lens_ref[s]

    def attend(r, rows, bias):
        n = rows.shape[0]
        keys, values = rows[:, :HD], rows[:, HD:]
        keys = jnp.concatenate([keys, keys], axis=1)
        values = jnp.concatenate([values, jnp.ones((n, HD), BF16)], axis=1)

        def scores(h):
            return lax.dot_general(q_scaled[r, h], keys, NT, preferred_element_type=F32) + bias

        now_scores = scores(0)
        for h in range(HEADS):
            ahead = scores(h + 1) if h + 1 < HEADS else None
            before = tops[r, h]
            now = jnp.maximum(before, jnp.max(now_scores, axis=-1, keepdims=True))
            p = jnp.exp2(now_scores - jnp.concatenate([now] * (n // HD), axis=1)).astype(BF16)
            shrink = jnp.exp2(before - now)
            tops[r, h] = now
            o = jnp.dot(p, values, preferred_element_type=F32)
            acc[r, h] = acc[r, h] * jnp.concatenate([shrink, shrink], axis=1) + o
            now_scores = ahead

    def near_step(r, yp, zc):
        key_at = ((2 * big + zc) * NY + yp) * BLOCK
        row_at = ((2 * big + r) * NY + y) * BLOCK + k * ROWS
        row = row_at + lax.broadcasted_iota(jnp.int32, (ROWS, BLOCK), 0)
        col = key_at + lax.broadcasted_iota(jnp.int32, (ROWS, BLOCK), 1)
        bias = jnp.where(col < jnp.minimum(row + 1, length), 0.0, NEG)
        attend(r, blocks[big, yp, zc].reshape(BLOCK, 2 * HD), bias)

    def far_step(r, yp):
        attend(r, blocks[0, yp].reshape(2 * BLOCK, 2 * HD), 0.0)

    lane = lax.broadcasted_iota(jnp.int32, (32, HD), 1)

    def packed(top, sums):
        return jnp.where(lane < HD // 2, top, sums)

    def merge(buf, n):
        m = [buf[i, 1][:, :1] for i in range(n)]
        l = [buf[i, 1][:, HD - 1 :] for i in range(n)]
        top = functools.reduce(jnp.maximum, m)
        w = [jnp.exp(t - top) for t in m]
        sums = sum(a * b for a, b in zip(l, w))
        o = sum(buf[i, 0] * w[i] for i in range(n))
        return top, sums, o

    def tree(buf, n):
        parts = [buf[i] for i in range(n)]
        while len(parts) > 1:
            parts = [parts[i] + parts[i + 1] for i in range(0, len(parts), 2)]
        return parts[0]

    def decode_1():
        gathered(proj_row, row_peer, 2 * y + k, ROW - 1, peer_send, 0, pr_recv)
        proj_z[z] = tree(proj_row, ROW)
        spread(proj_z, z_peer, z, 3, peer_send, 7, pz_recv)

    def decode_2():
        gathered(proj_z, z_peer, z, 3, peer_send, 7, pz_recv)
        total = tree(proj_z, NZ)
        proj = total[:, : 6 * HD] * lax.rsqrt(total[:, 6 * HD :][:, :1] / width + EPS)
        sub = lax.broadcasted_iota(jnp.int32, (8, HD), 0)
        position = jnp.where(sub % 2 == 0, lens_ref[0], lens_ref[1]) + sub // 2
        angle = position.astype(F32) * freq_ref[...]
        cosine, sine = jnp.cos(angle), jnp.sin(angle)
        sine = jnp.where(lax.broadcasted_iota(jnp.int32, (8, HD), 1) < HD // 2, -sine, sine)

        def rotated(v):
            return (v * cosine + pltpu.roll(v, HD // 2, 1) * sine).astype(BF16)

        queries = jnp.concatenate([rotated(proj[:, h * HD : (h + 1) * HD]) for h in range(HEADS)], axis=0)
        blank = jnp.zeros((HD - 8, HD), F32)
        new_key = jnp.concatenate([rotated(proj[:, 4 * HD : 5 * HD]).astype(F32), blank], axis=0).astype(BF16)
        new_value = jnp.concatenate([proj[:, 5 * HD : 6 * HD], blank], axis=0).astype(BF16)
        own = kv_own[...].reshape(2 * ROWS, 2 * HD)
        keys = jnp.concatenate([own[:, :HD], new_key], axis=0)
        values = jnp.concatenate([own[:, HD:], new_value], axis=0)
        scores = lax.dot_general(queries, keys, NT, preferred_element_type=F32) * (1.0 / math.sqrt(HD))
        row = lax.broadcasted_iota(jnp.int32, scores.shape, 0) % 8
        col = lax.broadcasted_iota(jnp.int32, scores.shape, 1)
        new = col - 2 * ROWS
        limit = jnp.where(col < ROWS, lens_ref[0], lens_ref[1])
        old_ok = (col < 2 * ROWS) & (col // ROWS == row % 2) & (seq * ROWS + col % ROWS < limit)
        new_ok = (new >= 0) & (new <= row) & (new % 2 == row % 2) & (seq == 0)
        scores = jnp.where(old_ok | new_ok, scores, NEG)
        top = jnp.max(scores, axis=-1, keepdims=True)
        p = jnp.exp(scores - top)
        mine = 2 * y + k
        soft_row[mine, 0] = jnp.dot(p.astype(BF16), values, preferred_element_type=F32)
        soft_row[mine, 1] = packed(top, jnp.sum(p, axis=-1, keepdims=True))
        spread(soft_row, row_peer, mine, ROW - 1, peer_send, 10, sr_recv)

    def decode_3():
        gathered(soft_row, row_peer, 2 * y + k, ROW - 1, peer_send, 10, sr_recv)
        top, sums, o = merge(soft_row, ROW)
        soft_z[z, 0] = o
        soft_z[z, 1] = packed(top, sums)
        spread(soft_z, z_peer, z, 3, peer_send, 17, sz_recv)

    def decode_4():
        gathered(soft_z, z_peer, z, 3, peer_send, 17, sz_recv)
        _, sums, o = merge(soft_z, NZ)
        att = o / sums
        out = jnp.zeros((8, ROWS), F32)
        for h in range(HEADS):
            head = att[8 * h : 8 * h + 8].astype(BF16)
            out += jnp.dot(head, wout[h * HD : (h + 1) * HD, :], preferred_element_type=F32)
        out_tp[tp] = out
        spread(out_tp, tp_peer, tp, N_TP - 1, peer_send, 20, ot_recv)

    def decode_5():
        gathered(out_tp, tp_peer, tp, N_TP - 1, peer_send, 20, ot_recv)
        dec_ref[...] = (hid + tree(out_tp, N_TP)).astype(BF16)

    def far_first(zc):
        @pl.when(big == 1)
        def _():
            arrived(0, y, zc)
            hand_out(0, zc)

    def far_pass_on():
        @pl.when(big == 1)
        def _():
            pass_on(0, 0)
            pass_on(0, 1)

    def far_take(*which):
        @pl.when(big == 1)
        def _():
            for yp, zc in which:
                take(0, yp, zc)

    def by(i, values):
        out = values[-1]
        for j in range(len(values) - 2, -1, -1):
            out = jnp.where(i == j, values[j], out)
        return out

    def result(r, h):
        return (acc[r, h][:, :HD] / acc[r, h][:, HD:]).astype(BF16)

    back = copy(o_out, o_in, swap_send.at[2], swap_recv.at[1], pair)

    near_2 = 8 + EARLY
    far_2 = near_2 + 8
    far_3 = far_2 + NY

    @pl.loop(0, far_3 + NY - EARLY)
    def _(i):
        @pl.when(i == 1)
        def _():
            arrived(big, y, 1 - s)
            hand_out(big, 1 - s)

        @pl.when(i == 2)
        def _():
            pass_on(big, 0)
            pass_on(big, 1)

        @pl.when(i == 4)
        def _():
            take(big, y_minus, 1)
            take(big, y_plus, 0)
            far_first(s)
            decode_1()

        @pl.when(i == 6)
        def _():
            take(big, y_far, 0)
            take(big, y_far, 1)
            far_first(1 - s)

        @pl.when(i == 8)
        def _():
            decode_2()

        @pl.when(i == near_2)
        def _():
            far_pass_on()
            swap_q.wait_recv()
            scale_queries(q_in, 1 - s)

        @pl.when(i == near_2 + 2)
        def _():
            far_take((y_minus, 1), (y_plus, 0))

        @pl.when(i == near_2 + 4)
        def _():
            decode_3()

        @pl.when(i == near_2 + 6)
        def _():
            far_take((y_far, 0), (y_far, 1))

            @pl.loop(1, N_SEQ)
            def _(d):
                page(lax.rem(seq + d, N_SEQ), seq).start()

        @pl.when(i == far_2 + 1)
        def _():
            loads[4].wait()
            decode_4()

        @pl.when(i == far_3)
        def _():
            for h in range(HEADS):
                o_out[:, h * HD : (h + 1) * HD] = result(1 - s, h)
            back.start()

        j = jnp.where(i < 8, i, i - near_2)
        yp = lax.rem(y + by(j, [0, 0, 3, 1, 3, 1, 2, 2]), NY)
        zc = by(j, [s, 1 - s, 0, 1, 1, 0, 0, 1])
        r = jnp.where(i < 8, s, 1 - s)

        @pl.when(i < 8)
        def _():
            mate_arrived(big, yp, zc)

        @pl.when((i < 8) | ((i >= near_2) & (i < far_2)))
        def _():
            @pl.when(zc * NY + yp <= r * NY + y)
            def _():
                near_step(r, yp, zc)

        place = jnp.where(i < near_2, i - 8, jnp.where(i < far_3, i - far_2, i - far_3 + EARLY))
        far_yp = lax.rem(y + by(place, [0, 3, 1, 2]), NY)
        again = (i >= far_2) & (i < far_2 + EARLY) | (i >= far_3)
        early = (i >= 8) & (i < near_2)

        @pl.when((big == 1) & (early | (i >= far_2)))
        def _():
            @pl.when(jnp.logical_not(again))
            def _():
                mate_arrived(0, far_yp, 0)
                mate_arrived(0, far_yp, 1)

            far_step(jnp.where((i >= far_2) & (i < far_3), 1 - s, s), far_yp)

    for h in range(HEADS):
        attn_ref[s, :, h * HD : (h + 1) * HD] = result(s, h)
    decode_5()

    swap_kv.wait_send()
    swap_q.wait_send()
    own_page.wait()

    @pl.loop(1, N_SEQ)
    def _(d):
        page(lax.rem(seq + d, N_SEQ), lax.rem(seq + d, N_SEQ)).wait()

    pages_ref[...] = pages[...]

    @pl.loop(0, 2)
    def _(zp):
        @pl.when(zp <= big)
        def _():
            for zc in (0, 1):
                for direction in (0, 1):
                    first(zp, direction, zc).wait_send()
                for yp in range(NY):
                    to_mate(zp, yp, zc).wait_send()
                forward(zp, zc).wait_send()

    @pl.when(big == 0)
    def _():
        far(0).wait_send()
        far(1).wait_send()

    back.wait()
    attn_ref[1 - s] = o_in[...]


def publish(attn_ref, pages_ref, dec_ref, attn_out, pages_out, dec_out, leave):
    pieces = [(attn_ref.at[0], attn_out.at[0]), (attn_ref.at[1], attn_out.at[1]), (pages_ref, pages_out)]
    outward = [pltpu.make_async_copy(src, dst, leave.at[i]) for i, (src, dst) in enumerate(pieces)]
    for c in outward:
        c.start()
    for i in range(dec_out.shape[0]):
        dec_out[i] = dec_ref[2 * i : 2 * i + 2, :]
    for c in outward:
        c.wait()


def on_device(q_prefill, kv_prefill, prompt_len, group_of, hidden, norm_gain, w_qkv, w_out):
    n_prompts, rows = q_prefill.shape[:2]
    cycle = lax.axis_size("seq")
    steps = hidden.shape[0]
    frequency = BASE ** (-2.0 * np.arange(HD // 2, dtype=np.float64) / HD)
    frequency = np.concatenate([frequency, frequency])[None].astype(np.float32)

    vmem = pl.BlockSpec(memory_space=pltpu.VMEM)
    smem = pl.BlockSpec(memory_space=pltpu.SMEM)
    hbm = pl.BlockSpec(memory_space=pltpu.HBM)
    dma = pltpu.SemaphoreType.DMA
    width = hidden.shape[2] * cycle
    attn, pages, decoded = pl.pallas_call(
        functools.partial(kernel, float(width)),
        out_shape=(
            pltpu.VMEM((n_prompts, rows, HEADS * HD), BF16),
            pltpu.VMEM((N_SEQ, PIECE, 2 * HD), BF16),
            pltpu.VMEM((steps * n_prompts, rows), BF16),
        ),
        in_specs=[smem, smem, hbm, hbm, vmem, vmem, hbm, hbm, vmem],
        out_specs=(vmem, vmem, vmem),
        scratch_shapes=[
            pltpu.VMEM((2, NY, 2, 2, ROWS, 2 * HD), BF16),
            pltpu.VMEM((2, ROWS, 2 * HD), BF16),
            pltpu.VMEM((ROWS, HEADS * HD), BF16),
            pltpu.VMEM((ROWS, HEADS * HD), BF16),
            pltpu.VMEM((ROWS, 6 * HD), BF16),
            pltpu.VMEM((HEADS * HD, ROWS), BF16),
            pltpu.VMEM((2, HEADS, ROWS, 2 * HD), BF16),
            pltpu.VMEM((2, HEADS, ROWS, 2 * HD), F32),
            pltpu.VMEM((2, HEADS, ROWS, HD), F32),
            pltpu.VMEM((ROWS, HEADS * HD), BF16),
            pltpu.VMEM((ROWS, HEADS * HD), BF16),
            pltpu.VMEM((ROW, 8, 7 * HD), F32),
            pltpu.VMEM((NZ, 8, 7 * HD), F32),
            pltpu.VMEM((ROW, 2, 32, HD), F32),
            pltpu.VMEM((NZ, 2, 32, HD), F32),
            pltpu.VMEM((N_TP, 8, ROWS), F32),
            pltpu.VMEM((2, N_SEQ // 2, PIECE, 2 * HD), BF16),
            pltpu.VMEM((N_SEQ, PIECE, 2 * HD), BF16),
            dma((6,)), dma((3,)), dma((2,)), dma((2, NY, 2)), dma((2, NY, 2)),
            dma((2, 2, 2)), dma((2, 2)), dma((2, NY, 2)), dma((2,)),
            dma((27,)), dma((ROW,)), dma((NZ,)), dma((ROW,)), dma((NZ,)), dma((N_TP,)),
            dma((N_SEQ,)), dma((N_SEQ,)),
        ],
        compiler_params=pltpu.CompilerParams(
            collective_id=0, has_side_effects=True, vmem_limit_bytes=60 * 1024 * 1024
        ),
        cost_estimate=pl.CostEstimate(flops=9 * 10**9, bytes_accessed=3 * 10**6, transcendentals=17 * 10**6),
    )(
        prompt_len,
        group_of,
        q_prefill.reshape(n_prompts, rows, HEADS * HD),
        kv_prefill.reshape(n_prompts, rows, 2 * HD),
        hidden,
        norm_gain.reshape(1, rows),
        w_qkv.reshape(rows, 6 * HD),
        w_out.reshape(HEADS * HD, rows),
        frequency,
    )
    attn, pages, decoded = pl.pallas_call(
        publish,
        out_shape=(
            jax.ShapeDtypeStruct(attn.shape, BF16),
            jax.ShapeDtypeStruct(pages.shape, BF16),
            jax.ShapeDtypeStruct(hidden.shape, BF16),
        ),
        in_specs=[vmem, vmem, vmem],
        out_specs=(hbm, hbm, vmem),
        scratch_shapes=[dma((3,))],
        compiler_params=pltpu.CompilerParams(vmem_limit_bytes=16 * 1024 * 1024),
    )(attn, pages, decoded)
    return (
        attn.reshape(n_prompts, rows, 1, HEADS * HD),
        pages.reshape(N_SEQ * PIECE, 1, 2 * HD),
        decoded,
    )


def solution(mesh):
    placed = (
        P(None, "seq", "tp", None),
        P(None, "seq", "tp", None),
        P(),
        P(),
        P(None, None, "seq"),
        P("seq"),
        P("seq", "tp", None),
        P("tp", None, "seq"),
    )
    return jax.shard_map(
        on_device,
        mesh=mesh,
        in_specs=placed,
        out_specs=(P(None, "seq", "tp", None), P("seq", "tp", None), P(None, None, "seq")),
        check_vma=False,
    )
```
